32 devices in a mesh: batch: 8 (over z, x), tensor: 4 (over y, core).
Axes of the slice: x: 2, y: 2, z: 4, core: 2. Of those that a mesh axis runs over, the one named last changes fastest.
Arguments:
- hidden_in: bfloat16 [4096, 8192], P('batch', 'tensor'), may hold values from -1600 to 1600, as said below
- norm_gain: bfloat16 [8192], P('tensor'), may hold values from 0.099609375 to 1.8984375
- q_weight: bfloat16 [8192, 4096], P(('batch', 'tensor')), may hold values from -0.4087961 to 0.4087961, as said below
- k_weight: bfloat16 [8192, 512], P(('batch', 'tensor')), may hold values from -0.044194174 to 0.044194174, as said below
- v_weight: bfloat16 [8192, 512], P(('batch', 'tensor')), may hold values from -0.0625 to 0.0625
Outputs:
- head_out: bfloat16 [4096, 4096], P('batch', 'tensor')
The draws below stay inside these ranges and needn't reach their ends.
Inputs may be any that keep to these rules, and one draw needn't show every extreme that they name: `hidden_in`: activations with independent scales over rows and over features. `q_weight`: A dense matrix. `k_weight`: A dense matrix.
All inputs are finite; a program needn't handle non-finite values.
Results may differ from the reference program's by a relative error of at most 0.008.
Values may be sent and summed in bfloat16 or wider, within the bound.
No kernel may reach another device: no remote copies, remote signals or barrier semaphores. Data moves between devices by JAX's collectives and lax.ppermute only.
A program may use at most 128 MiB of HBM per device.

```python
import math
import jax
import jax.numpy as jnp
from jax import lax

D = 8192
HD = 128
QH = 32
KVH = 4
SEQ = 512
TOKENS = 4096


def draw_hidden_in(key, part):
    key_base = jax.random.fold_in(key, 11)
    key_rows = jax.random.fold_in(key, 12)
    key_cols = jax.random.fold_in(key, 13)
    row_scale = jnp.exp(jax.random.uniform(key_rows, (TOKENS, 1), jnp.float32, 0.0, math.log(10.0)))
    ramp = 1.0 + 2.0 * jnp.arange(D, dtype=jnp.float32)[None, :] / (D - 1)
    col_scale = ramp * jnp.exp(jax.random.uniform(key_cols, (1, D), jnp.float32, 0.0, math.log(10.0)))
    base = jnp.clip(jax.random.normal(key_base, (TOKENS, D), jnp.float32), -5.0, 5.0)
    return (base * row_scale * col_scale).astype(jnp.bfloat16)


def shared_keys(key):
    key_main = jax.random.fold_in(key, 31)
    values = jnp.clip(jax.random.normal(key_main, (D, KVH * HD), jnp.float32), -4.0, 4.0)
    return values / jnp.sqrt(jnp.float32(D))


def draw_k_weight(key, part):
    return shared_keys(key).astype(jnp.bfloat16)


def draw_q_weight(key, part):
    key_main = jax.random.fold_in(key, 21)
    values = jnp.clip(jax.random.normal(key_main, (D, QH * HD), jnp.float32), -4.0, 4.0)
    return (values / jnp.sqrt(jnp.float32(D))).astype(jnp.bfloat16)


def block_scale(rng, dims, cuts, least, high):
    def one(axis_at, blocks):
        draws = jax.random.uniform(jax.random.fold_in(jax.random.fold_in(rng, 6), axis_at), (blocks,), jnp.float32, least / len(cuts), high / len(cuts))
        return jnp.repeat(jnp.exp(draws), dims[axis_at] // blocks).reshape((-1,) + (1,) * (len(dims) - axis_at - 1))

    gain = one(*cuts[0])
    for cut in cuts[1:]:
        gain = gain * one(*cut)
    return gain


def normal_values(key, extent, deviation, bound, cuts=(), held_as=jnp.bfloat16):
    values = jax.random.normal(key, extent, jnp.float32) * deviation
    if len(cuts) > 0:
        values = block_scale(key, extent, cuts, -0.22, 0.18) * values
    return jnp.clip(values, min=-bound, max=bound).astype(held_as)


def setup_inputs(seed: int = 0) -> dict:
    splits = jax.random.split(jax.random.key(seed), 6)
    return {
        "hidden_in": draw_hidden_in(jax.random.fold_in(splits[5], 71), 0),
        "norm_gain": jnp.clip(1.0 + 0.18 * jax.random.normal(splits[1], (D,), jnp.float32), 0.099609375, 1.8984375).astype(jnp.bfloat16),
        "q_weight": draw_q_weight(jax.random.fold_in(splits[5], 71), 0),
        "k_weight": draw_k_weight(jax.random.fold_in(splits[5], 71), 0),
        "v_weight": normal_values(splits[4], (D, KVH * HD), D ** -0.5, 0.0625, ((0, 32),)),
    }


def rotate(field):
    half = field.shape[-1] // 2
    position = jnp.arange(field.shape[1], dtype=jnp.float32)
    freqs = 500000.0 ** (-(jnp.arange(half, dtype=jnp.float32) * 2.0) / field.shape[-1])
    angles = position[:, None] * freqs[None, :]
    cosine = jnp.cos(angles)[None, :, None, :]
    sine = jnp.sin(angles)[None, :, None, :]
    first = field[..., :half]
    second = field[..., half:]
    return jnp.concatenate([first * cosine - second * sine, second * cosine + first * sine], axis=-1)

def reference(hidden_in, norm_gain, q_weight, k_weight, v_weight):
    values = hidden_in.astype(jnp.float32)
    meansq = lax.optimization_barrier(jnp.mean(values * values, axis=-1, keepdims=True))
    normed = (values * lax.rsqrt(meansq + 1e-05) * norm_gain.astype(jnp.float32)).astype(jnp.bfloat16)
    q_lin = jnp.dot(normed, q_weight, preferred_element_type=jnp.float32)
    k_lin = jnp.dot(normed, k_weight, preferred_element_type=jnp.float32)
    v_lin = jnp.dot(normed, v_weight, preferred_element_type=jnp.float32)
    q_rot = rotate(q_lin.reshape(-1, SEQ, QH, HD)).astype(jnp.bfloat16)
    k_rot = rotate(k_lin.reshape(-1, SEQ, KVH, HD)).astype(jnp.bfloat16)
    v_all = v_lin.astype(jnp.bfloat16).reshape(-1, SEQ, KVH, HD)
    group = QH // KVH
    causal = jnp.tril(jnp.ones((SEQ, SEQ), dtype=bool))

    def attend(items):
        queries, keys, vals = items
        keys_wide = jnp.repeat(keys, group, axis=1).astype(jnp.float32)
        vals_wide = jnp.repeat(vals, group, axis=1).astype(jnp.float32)
        scores = jnp.einsum('shd,thd->hst', queries.astype(jnp.float32), keys_wide) / jnp.sqrt(jnp.float32(HD))
        scores = jnp.where(causal[None], scores, jnp.float32(-1e+30))
        top = lax.optimization_barrier(jnp.max(scores, axis=-1, keepdims=True))
        expo = jnp.exp(scores - top)
        probs = (expo / lax.optimization_barrier(jnp.sum(expo, axis=-1, keepdims=True))).astype(jnp.bfloat16)
        result = jnp.einsum('hst,thd->shd', probs.astype(jnp.float32), vals_wide)
        return result.astype(jnp.bfloat16).reshape(SEQ, QH * HD)
    outputs = lax.map(attend, (q_rot, k_rot, v_all))
    return outputs.reshape(-1, QH * HD)
```

```python
import jax
import jax.numpy as jnp
from jax import lax
from jax.sharding import PartitionSpec as P

HD = 128
AXES = ("batch", "tensor")


def rotary_tables(seq_len, head_size):
    half = head_size // 2
    position = jnp.arange(seq_len, dtype=jnp.float32)
    freqs = 500000.0 ** (-(jnp.arange(half, dtype=jnp.float32) * 2.0) / head_size)
    angles = position[:, None] * freqs[None, :]
    return jnp.cos(angles), jnp.sin(angles)


def rotate_heads(field, tables):
    seq_len = field.shape[0]
    shaped = field.reshape(seq_len, -1, HD)
    half = HD // 2
    cosine = tables[0][:, None, :]
    sine = tables[1][:, None, :]
    first = shaped[..., :half]
    second = shaped[..., half:]
    turned = jnp.concatenate(
        [first * cosine - second * sine, second * cosine + first * sine], axis=-1
    )
    return turned.astype(jnp.bfloat16)


def attend(q_rot, k_rot, v_val):
    seq_len = q_rot.shape[0]
    scores = jnp.einsum("shd,td->hst", q_rot, k_rot, preferred_element_type=jnp.float32) / jnp.sqrt(
        jnp.float32(HD)
    )
    causal = jnp.tril(jnp.ones((seq_len, seq_len), dtype=bool))
    scores = jnp.where(causal[None], scores, jnp.float32(-1e30))
    top = jnp.max(scores, axis=-1, keepdims=True)
    expo = jnp.exp(scores - top)
    probs = (expo / jnp.sum(expo, axis=-1, keepdims=True)).astype(jnp.bfloat16)
    result = jnp.einsum("hst,td->shd", probs, v_val, preferred_element_type=jnp.float32)
    return result.astype(jnp.bfloat16).reshape(seq_len, -1)


def gathered_plan(hidden_in, norm_gain, q_weight, k_weight, v_weight):
    tensor_count = lax.axis_size("tensor")
    whole_rows, whole_gain = (
        lax.all_gather(hidden_in, "tensor", axis=1, tiled=True),
        lax.all_gather(norm_gain, "tensor", axis=0, tiled=True),
    )
    values = whole_rows.astype(jnp.float32)
    meansq = jnp.mean(values * values, axis=-1, keepdims=True)
    normed = (values * lax.rsqrt(meansq + 1e-05) * whole_gain.astype(jnp.float32)).astype(
        jnp.bfloat16
    )
    own_rows = q_weight.shape[0]
    kv_heads = k_weight.shape[1] // HD
    repeat_count = tensor_count // kv_heads
    q_send = q_weight.reshape(own_rows, tensor_count, -1)
    k_send = jnp.repeat(k_weight.reshape(own_rows, kv_heads, HD), repeat_count, axis=1)
    v_send = jnp.repeat(v_weight.reshape(own_rows, kv_heads, HD), repeat_count, axis=1)
    sends = jnp.concatenate([k_send, v_send, q_send], axis=2)
    recv = lax.all_to_all(sends, "tensor", split_axis=1, concat_axis=0, tiled=True)
    full = lax.all_gather(recv.reshape(-1, recv.shape[2]), "batch", axis=0, tiled=True)
    lin = jnp.dot(normed, full, preferred_element_type=jnp.float32)
    tables = rotary_tables(normed.shape[0], HD)
    k_rot = rotate_heads(lin[:, :HD], tables)[:, 0, :]
    v_val = lin[:, HD : 2 * HD].astype(jnp.bfloat16)
    return attend(rotate_heads(lin[:, 2 * HD :], tables), k_rot, v_val)


def move(value, route):
    pairs = []
    for flat in range(32):
        to = route(flat >> 3, flat >> 2 & 1, flat >> 1 & 1, flat & 1)
        if to is not None:
            pairs.append((flat, ((to[0] * 2 + to[1]) * 2 + to[2]) * 2 + to[3]))
    return lax.ppermute(value, AXES, pairs)


def swap_x(z, x, y, c):
    return z, 1 - x, y, c


def swap_y(z, x, y, c):
    return z, x, 1 - y, c


def swap_xy(z, x, y, c):
    return z, 1 - x, 1 - y, c


def swap_c(z, x, y, c):
    return z, x, y, 1 - c


def swap_near(z, x, y, c):
    return z ^ 1, x, y, c


def swap_far(z, x, y, c):
    return z ^ 2, x, y, c


def pick(pair, index):
    return lax.dynamic_index_in_dim(pair, index, 0, keepdims=False)


CHUNKS = ((0, 2), (2, 4), (4, 6), (6, 8))


def split_plan(hidden_in, norm_gain, q_weight, k_weight, v_weight):
    flat = lax.axis_index(AXES)
    z, x, y, c = flat >> 3, flat >> 2 & 1, flat >> 1 & 1, flat & 1
    odd = z & 1
    home = c == odd
    rows = hidden_in.shape[0]
    own = q_weight.shape[0]
    q_cols = q_weight.shape[1] // 4

    def columns(group, lo, hi):
        take = lax.dynamic_slice_in_dim
        q_part = take(q_weight, group * q_cols + lo * HD, (hi - lo) * HD, 1)
        if lo > 0:
            return q_part
        return jnp.concatenate(
            [take(k_weight, group * HD, HD, 1), take(v_weight, group * HD, HD, 1), q_part], axis=1
        )

    near, far = [], []
    for lo, hi in CHUNKS:
        mine = columns(2 * y + x, lo, hi)
        from_x = move(columns(2 * y + 1 - x, lo, hi), swap_x)
        from_y = move(columns(2 * (1 - y) + x, lo, hi), swap_y)
        from_xy = move(columns(2 * (1 - y) + 1 - x, lo, hi), swap_xy)
        block = jnp.zeros((4,) + mine.shape, mine.dtype)
        for piece, px, py in (
            (mine, x, y), (from_x, 1 - x, y), (from_y, x, 1 - y), (from_xy, 1 - x, 1 - y)
        ):
            block = lax.dynamic_update_index_in_dim(block, piece, 2 * px + py, 0)
        block = block.reshape(4 * own, -1)
        near.append(block)
        far.append(move(block, swap_far))

    values = hidden_in.astype(jnp.float32)
    total = jnp.sum(values * values, axis=-1)
    total = total + move(total, swap_c)
    total = total + move(total, swap_y)
    scale = lax.rsqrt(total / (4 * hidden_in.shape[1]) + 1e-05)
    normed = (values * scale[:, None] * norm_gain.astype(jnp.float32)[None, :]).astype(jnp.bfloat16)

    halves = normed.reshape(rows, 4, 2, own).transpose(2, 0, 1, 3).reshape(2, rows, 4 * own)
    half_same, half_other = pick(halves, odd), pick(halves, 1 - odd)

    def to_same_parity(z, x, y, c):
        return (z, x, y, 1 - c) if c == z & 1 else (z ^ 1, x, y, c)

    def to_other_plane(z, x, y, c):
        return None if c == z & 1 else (z ^ 1, x, y, 1 - c)

    got_one = move(half_other, to_same_parity)
    got_two = move(half_same, to_other_plane)
    here = jnp.stack(
        [jnp.where(home, half_same, got_one), jnp.where(home, got_one, got_two)]
    )
    here_x = move(here, swap_x)
    here_y = move(here, swap_y)
    here_xy = jnp.stack([move(here_x[0], swap_y), move(here_y[1], swap_x)])
    by_y = (jnp.stack([here, here_x]), jnp.stack([here_y, here_xy]))
    straight = y == z >> 1
    x_near = jnp.where(straight, by_y[0], by_y[1]).reshape(4 * rows, -1)
    x_far = jnp.where(straight, by_y[1], by_y[0]).reshape(4 * rows, -1)

    tables = rotary_tables(rows, HD)
    keep = c ^ x
    results = []
    k_rot = v_val = None
    for j, (lo, hi) in enumerate(CHUNKS):
        part = jnp.dot(x_near, near[j], preferred_element_type=jnp.float32)
        part = part + jnp.dot(x_far, far[j], preferred_element_type=jnp.float32)
        part = part.reshape(2, 2, rows, -1)
        both = pick(part, keep) + move(pick(part, 1 - keep), swap_c)
        sent = both[1] if lo == 0 else both[1].astype(jnp.float16)
        lin = both[0] + move(sent, swap_near).astype(jnp.float32)
        if lo == 0:
            k_rot = rotate_heads(lin[:, :HD], tables)[:, 0, :]
            v_val = lin[:, HD : 2 * HD].astype(jnp.bfloat16)
            lin = lin[:, 2 * HD :]
        out = attend(rotate_heads(lin, tables), k_rot, v_val)

        def to_owner(z, x, y, c):
            return None if x == c else (z, c, y, x)

        results.append(jnp.where(x == c, out, move(out, to_owner)))
    return jnp.concatenate(results, axis=1)


def solution(mesh):
    placed = (
        P("batch", "tensor"),
        P("tensor"),
        P(("batch", "tensor"), None),
        P(("batch", "tensor"), None),
        P(("batch", "tensor"), None),
    )
    plan = split_plan if dict(mesh.shape) == {"batch": 8, "tensor": 4} else gathered_plan
    return jax.shard_map(
        plan, mesh=mesh, in_specs=placed, out_specs=P("batch", "tensor"), check_vma=False
    )
```

```python
import jax
import jax.numpy as jnp
from jax import lax
from jax.experimental import pallas as pl
from jax.experimental.pallas import tpu as pltpu
from jax.sharding import PartitionSpec as P

HD = 128
AXES = ("batch", "tensor")


def rotary_tables(seq_len, head_size):
    half = head_size // 2
    position = jnp.arange(seq_len, dtype=jnp.float32)
    freqs = 500000.0 ** (-(jnp.arange(half, dtype=jnp.float32) * 2.0) / head_size)
    angles = position[:, None] * freqs[None, :]
    return jnp.cos(angles), jnp.sin(angles)


def rotate_heads(field, tables):
    seq_len = field.shape[0]
    shaped = field.reshape(seq_len, -1, HD)
    half = HD // 2
    cosine = tables[0][:, None, :]
    sine = tables[1][:, None, :]
    first = shaped[..., :half]
    second = shaped[..., half:]
    turned = jnp.concatenate(
        [first * cosine - second * sine, second * cosine + first * sine], axis=-1
    )
    return turned.astype(jnp.bfloat16)


def attend(q_rot, k_rot, v_val):
    seq_len = q_rot.shape[0]
    scores = jnp.einsum("shd,td->hst", q_rot, k_rot, preferred_element_type=jnp.float32) / jnp.sqrt(
        jnp.float32(HD)
    )
    causal = jnp.tril(jnp.ones((seq_len, seq_len), dtype=bool))
    scores = jnp.where(causal[None], scores, jnp.float32(-1e30))
    top = jnp.max(scores, axis=-1, keepdims=True)
    expo = jnp.exp(scores - top)
    probs = (expo / jnp.sum(expo, axis=-1, keepdims=True)).astype(jnp.bfloat16)
    result = jnp.einsum("hst,td->shd", probs, v_val, preferred_element_type=jnp.float32)
    return result.astype(jnp.bfloat16).reshape(seq_len, -1)


def gathered_plan(hidden_in, norm_gain, q_weight, k_weight, v_weight):
    tensor_count = lax.axis_size("tensor")
    whole_rows, whole_gain = (
        lax.all_gather(hidden_in, "tensor", axis=1, tiled=True),
        lax.all_gather(norm_gain, "tensor", axis=0, tiled=True),
    )
    values = whole_rows.astype(jnp.float32)
    meansq = jnp.mean(values * values, axis=-1, keepdims=True)
    normed = (values * lax.rsqrt(meansq + 1e-05) * whole_gain.astype(jnp.float32)).astype(
        jnp.bfloat16
    )
    own_rows = q_weight.shape[0]
    kv_heads = k_weight.shape[1] // HD
    repeat_count = tensor_count // kv_heads
    q_send = q_weight.reshape(own_rows, tensor_count, -1)
    k_send = jnp.repeat(k_weight.reshape(own_rows, kv_heads, HD), repeat_count, axis=1)
    v_send = jnp.repeat(v_weight.reshape(own_rows, kv_heads, HD), repeat_count, axis=1)
    sends = jnp.concatenate([k_send, v_send, q_send], axis=2)
    recv = lax.all_to_all(sends, "tensor", split_axis=1, concat_axis=0, tiled=True)
    full = lax.all_gather(recv.reshape(-1, recv.shape[2]), "batch", axis=0, tiled=True)
    lin = jnp.dot(normed, full, preferred_element_type=jnp.float32)
    tables = rotary_tables(normed.shape[0], HD)
    k_rot = rotate_heads(lin[:, :HD], tables)[:, 0, :]
    v_val = lin[:, HD : 2 * HD].astype(jnp.bfloat16)
    return attend(rotate_heads(lin[:, 2 * HD :], tables), k_rot, v_val)


def move(value, route):
    pairs = []
    for flat in range(32):
        to = route(flat >> 3, flat >> 2 & 1, flat >> 1 & 1, flat & 1)
        if to is not None:
            pairs.append((flat, ((to[0] * 2 + to[1]) * 2 + to[2]) * 2 + to[3]))
    return lax.ppermute(value, AXES, pairs)


def swap_x(z, x, y, c):
    return z, 1 - x, y, c


def swap_y(z, x, y, c):
    return z, x, 1 - y, c


def swap_xy(z, x, y, c):
    return z, 1 - x, 1 - y, c


def swap_c(z, x, y, c):
    return z, x, y, 1 - c


def swap_near(z, x, y, c):
    return z ^ 1, x, y, c


def swap_far(z, x, y, c):
    return z ^ 2, x, y, c


CHUNKS = ((0, 5), (5, 8), (8, 10))
VMEM = 16 * 2**20


def place():
    batch, tensor = lax.axis_index("batch"), lax.axis_index("tensor")
    return batch >> 1, batch & 1, tensor >> 1, tensor & 1


def pick(pair, index):
    return lax.dynamic_index_in_dim(pair, index, 0, keepdims=False)


def call(kernel, out_shape, scratch=(), flops=0, name=None):
    shapes = out_shape if isinstance(out_shape, (list, tuple)) else (out_shape,)
    size = sum(2 * s.size * s.dtype.itemsize for s in shapes)
    return pl.pallas_call(
        kernel,
        out_shape=out_shape,
        scratch_shapes=scratch,
        compiler_params=pltpu.CompilerParams(vmem_limit_bytes=VMEM),
        cost_estimate=pl.CostEstimate(flops=flops, bytes_accessed=size, transcendentals=0),
        name=name,
    )


def pack_kernel(q_ref, k_ref, v_ref, *outs):
    _, x, y, _ = place()
    q_cols = outs[0].shape[1] - 2 * HD
    for out, px, py in zip(outs, (x, 1 - x, x, 1 - x), (y, y, 1 - y, 1 - y)):
        group = 2 * py + px
        out[:, :HD] = k_ref[:, pl.ds(pl.multiple_of(group * HD, HD), HD)]
        out[:, HD : 2 * HD] = v_ref[:, pl.ds(pl.multiple_of(group * HD, HD), HD)]
        out[:, 2 * HD :] = q_ref[:, pl.ds(pl.multiple_of(group * q_cols, HD), q_cols)]


def rest_kernel(own_ref, a_ref, b_ref, c_ref, all_ref, *outs):
    own = a_ref.shape[0]
    for i, ref in enumerate((own_ref, a_ref, b_ref, c_ref)):
        all_ref[i * own : (i + 1) * own, :] = ref[...]
        for out, (lo, hi) in zip(outs, CHUNKS):
            if i > 0:
                out[(i - 1) * own : i * own, :] = ref[:, lo * HD : hi * HD]


def squares_kernel(rows_ref, out):
    value = rows_ref[...].astype(jnp.float32)
    total = jnp.sum(value * value, axis=1, keepdims=True)
    out[...] = jnp.transpose(jnp.broadcast_to(total, (total.shape[0], HD)))[: out.shape[0], :]


def stamp_kernel(rows_ref, gain_ref, own_ref, got_ref, out):
    rows, feats = rows_ref.shape
    out[:rows, :] = rows_ref[...]
    left = own_ref[...] + got_ref[...]
    parts = []
    for _ in range(3):
        part = left.astype(jnp.bfloat16).astype(jnp.float32)
        parts.append(part)
        left = left - part
    parts.append(jnp.zeros((left.shape[0], feats - 3 * rows), jnp.float32))
    tile = jnp.concatenate(parts, axis=1)
    at = lax.broadcasted_iota(jnp.int32, tile.shape, 0)
    tile = jnp.where(at == 0, gain_ref[...].astype(jnp.float32), tile)
    out[rows:, :] = jnp.concatenate([tile, tile], axis=0).astype(jnp.bfloat16)


def scale_kernel(here, by_x, by_y, by_xy, out):
    z, x, y, c = place()
    rows, feats = out.shape[0], here.shape[1]
    at = jnp.where(y == z >> 1, 0, feats)

    def fill(same, other):
        tiles = [ref[rows:, :].astype(jnp.float32) for ref in (same, other)]
        total = sum(tile[1:2, i * rows : (i + 1) * rows] for tile in tiles for i in range(3))
        scale = lax.rsqrt(total / (4 * feats) + 1e-05)
        scale = jnp.transpose(jnp.broadcast_to(scale, (HD, rows)))[:, :1]
        for ref, tile, to in ((same, tiles[0], at), (other, tiles[1], feats - at)):
            value = ref[:rows, :].astype(jnp.float32) * scale * tile[:1, :]
            out[:, pl.ds(pl.multiple_of(to, feats), feats)] = value.astype(jnp.bfloat16)

    @pl.when(c == x)
    def _():
        fill(here, by_y)

    @pl.when(c != x)
    def _():
        fill(by_x, by_xy)


def product_kernel(lo, hi, lhs, near_both, mine_both, rest, rest_core, out, near, far):
    _, x, y, c = place()
    own = mine_both.shape[1]
    depth = near.shape[0]
    span = slice(lo * HD, hi * HD)
    for core, others in ((c, rest), (1 - c, rest_core)):
        for i in range(4):
            px = x if i % 2 == 0 else 1 - x
            py = y if i < 2 else 1 - y
            at = pl.ds(pl.multiple_of((4 * px + 2 * py + core) * own, own), own)
            near[at, :] = near_both[core, i * own : (i + 1) * own, span]
            far[at, :] = mine_both[core, :, span] if i == 0 else others[(i - 1) * own : i * own, :]
    out[...] = jnp.dot(lhs[:, :depth], near[...], preferred_element_type=jnp.float32) + jnp.dot(
        lhs[:, depth:], far[...], preferred_element_type=jnp.float32
    )


def turn(value, cosine, sine):
    return (value * cosine + pltpu.roll(value, HD // 2, 1) * sine).astype(jnp.bfloat16)


def attend_kernel(with_kv, *refs):
    if with_kv:
        near_ref, got_ref, cos_ref, sin_ref, out_ref, k_ref, v_ref = refs
    else:
        near_ref, got_ref, cos_ref, sin_ref, k_ref, v_ref, out_ref = refs
    rows = near_ref.shape[0]
    cosine, sine = cos_ref[...], sin_ref[...]

    def head(h):
        return near_ref[:, h * HD : (h + 1) * HD] + got_ref[:, h * HD : (h + 1) * HD]

    if with_kv:
        k_ref[...] = turn(head(0), cosine, sine)
        v_ref[...] = head(1).astype(jnp.bfloat16)
    skip = 2 if with_kv else 0
    half = rows // 2
    scale = 1.0 / (HD**0.5)
    above = lax.broadcasted_iota(jnp.int32, (half, half), 1) > lax.broadcasted_iota(
        jnp.int32, (half, half), 0
    )
    for h in range(out_ref.shape[1] // HD):
        q = turn(head(h + skip), cosine, sine)
        for block in range(2):
            mine = q[block * half : (block + 1) * half]
            parts = []
            for other in range(block + 1):
                keys = k_ref[other * half : (other + 1) * half, :]
                s = lax.dot_general(
                    mine, keys, (((1,), (1,)), ((), ())), preferred_element_type=jnp.float32
                )
                s = s * scale
                parts.append(jnp.where(above, -1e30, s) if other == block else s)
            s = parts[0] if block == 0 else jnp.concatenate(parts, axis=1)
            expo = jnp.exp(s - jnp.max(s, axis=1, keepdims=True))
            probs = (expo / jnp.sum(expo, axis=1, keepdims=True)).astype(jnp.bfloat16)
            got = jnp.dot(
                probs, v_ref[: (block + 1) * half, :], preferred_element_type=jnp.float32
            )
            out_ref[block * half : (block + 1) * half, h * HD : (h + 1) * HD] = got.astype(
                jnp.bfloat16
            )


def split_plan(hidden_in, norm_gain, q_weight, k_weight, v_weight):
    z, x, y, c = place()
    home = c == z & 1
    direct = c == x
    rows, feats = hidden_in.shape
    own = q_weight.shape[0]
    cols = (q_weight.shape[1] + k_weight.shape[1] + v_weight.shape[1]) // 4
    bf16 = jnp.bfloat16

    mine, for_x, for_y, for_xy = call(
        pack_kernel, [jax.ShapeDtypeStruct((own, cols), bf16)] * 4, name="pack"
    )(q_weight, k_weight, v_weight)
    def to_other_plane(z, x, y, c):
        return None if c == z & 1 else (z ^ 1, x, y, x)

    def to_core(z, x, y, c):
        return (z, x, y, x) if c == z & 1 and c != x else None

    squares = call(squares_kernel, jax.ShapeDtypeStruct((8, rows), jnp.float32), name="squares")(
        hidden_in
    )
    stamped = call(stamp_kernel, jax.ShapeDtypeStruct((rows + 16, feats), bf16), name="stamp")(
        hidden_in, norm_gain[None, :], squares, move(squares, swap_c)
    )
    here_far = move(stamped, to_other_plane)
    far_mine = move(mine, swap_far)
    pieces = (move(for_x, swap_x), move(for_y, swap_y), move(for_xy, swap_xy))
    mine, far_mine, pieces, here_far, later = lax.optimization_barrier(
        (mine, far_mine, pieces, here_far, stamped)
    )

    widths = [(hi - lo) * HD for lo, hi in CHUNKS]
    near_all, *rest = call(
        rest_kernel,
        [jax.ShapeDtypeStruct((4 * own, cols), bf16)]
        + [jax.ShapeDtypeStruct((3 * own, n), bf16) for n in widths],
        name="rest",
    )(mine, *pieces)

    def give(dx, dy):
        return lambda z, x, y, c: (z, x ^ dx, y ^ dy, c) if c == x else None

    def spread(block):
        return (block, move(block, give(1, 0)), move(block, give(0, 1)), move(block, give(1, 1)))

    far_rest = [move(rest[0], swap_far)]
    far_rows = spread(here_far)
    here_near = jnp.where(home, later, move(later, to_core))

    def normed(blocks):
        shape = jax.ShapeDtypeStruct((rows, 2 * feats), bf16)
        return call(scale_kernel, shape, name="scale_rows")(*blocks)

    far_rows, here_near, far_rest[0], rest[1] = lax.optimization_barrier(
        (far_rows, here_near, far_rest[0], rest[1])
    )
    far_rest.append(move(rest[1], swap_far))
    near_rows = spread(here_near)
    rest[2], far_rest[1], far_rows = lax.optimization_barrier((rest[2], far_rest[1], far_rows))
    far_rest.append(move(rest[2], swap_far))
    far_rows = normed(far_rows)
    near_rows = normed(near_rows)

    cores = [[0, 1], [2, 3]]
    near_both = lax.all_gather(near_all, "tensor", axis_index_groups=cores)
    far_mine_both = lax.all_gather(far_mine, "tensor", axis_index_groups=cores)

    cosine, sine = rotary_tables(rows, HD)
    cosine = jnp.concatenate([cosine, cosine], axis=1)
    sine = jnp.concatenate([-sine, sine], axis=1)

    weights = [
        (near_both, far_mine_both, far_rest[j], move(far_rest[j], swap_c))
        for j in range(len(CHUNKS))
    ]

    def product(block, j):
        lo, hi = CHUNKS[j]
        n = (hi - lo) * HD
        return call(
            lambda *refs: product_kernel(lo, hi, *refs),
            jax.ShapeDtypeStruct((rows, n), jnp.float32),
            scratch=[pltpu.VMEM((feats, n), bf16)] * 2,
            name="product",
        )(block, *weights[j])

    def to_owner(z, x, y, c):
        return None if x == c else (z, c, y, x)

    sums = []
    for j, (lo, hi) in enumerate(CHUNKS):
        sent = product(far_rows, j)
        if lo == 0:
            v_got = move(sent[:, HD : 2 * HD], swap_near)
            sent = jnp.concatenate([sent[:, :HD], sent[:, 2 * HD :]], axis=1)
        got = move(sent.astype(jnp.float16), swap_near).astype(jnp.float32)
        if lo == 0:
            got = jnp.concatenate([got[:, :HD], v_got, got[:, HD:]], axis=1)
        sums.append(got)

    results = []
    k_rot = v_val = None
    for j, (lo, hi) in enumerate(CHUNKS):
        args = (product(near_rows, j), sums[j], cosine, sine)
        if lo == 0:
            out, k_rot, v_val = call(
                lambda *refs: attend_kernel(True, *refs),
                [jax.ShapeDtypeStruct((rows, (hi - lo - 2) * HD), bf16)]
                + [jax.ShapeDtypeStruct((rows, HD), bf16)] * 2,
                name="attend_first",
            )(*args)
        else:
            out = call(
                lambda *refs: attend_kernel(False, *refs),
                jax.ShapeDtypeStruct((rows, (hi - lo) * HD), bf16),
                name="attend",
            )(*args, k_rot, v_val)
        results.append(jnp.where(direct, out, move(out, to_owner)))
    return jnp.concatenate(results, axis=1)


def solution(mesh):
    placed = (
        P("batch", "tensor"),
        P("tensor"),
        P(("batch", "tensor"), None),
        P(("batch", "tensor"), None),
        P(("batch", "tensor"), None),
    )
    plan = split_plan if dict(mesh.shape) == {"batch": 8, "tensor": 4} else gathered_plan
    return jax.shard_map(
        plan, mesh=mesh, in_specs=placed, out_specs=P("batch", "tensor"), check_vma=False
    )
```

```python
import jax
import jax.numpy as jnp
from jax import lax
from jax.experimental import pallas as pl
from jax.experimental.pallas import tpu as pltpu
from jax.sharding import PartitionSpec as P

HD = 128
AXES = ("batch", "tensor")


def rotary_tables(seq_len, head_size):
    half = head_size // 2
    position = jnp.arange(seq_len, dtype=jnp.float32)
    freqs = 500000.0 ** (-(jnp.arange(half, dtype=jnp.float32) * 2.0) / head_size)
    angles = position[:, None] * freqs[None, :]
    return jnp.cos(angles), jnp.sin(angles)


def rotate_heads(field, tables):
    seq_len = field.shape[0]
    shaped = field.reshape(seq_len, -1, HD)
    half = HD // 2
    cosine = tables[0][:, None, :]
    sine = tables[1][:, None, :]
    first = shaped[..., :half]
    second = shaped[..., half:]
    turned = jnp.concatenate(
        [first * cosine - second * sine, second * cosine + first * sine], axis=-1
    )
    return turned.astype(jnp.bfloat16)


def attend(q_rot, k_rot, v_val):
    seq_len = q_rot.shape[0]
    scores = jnp.einsum("shd,td->hst", q_rot, k_rot, preferred_element_type=jnp.float32) / jnp.sqrt(
        jnp.float32(HD)
    )
    causal = jnp.tril(jnp.ones((seq_len, seq_len), dtype=bool))
    scores = jnp.where(causal[None], scores, jnp.float32(-1e30))
    top = jnp.max(scores, axis=-1, keepdims=True)
    expo = jnp.exp(scores - top)
    probs = (expo / jnp.sum(expo, axis=-1, keepdims=True)).astype(jnp.bfloat16)
    result = jnp.einsum("hst,td->shd", probs, v_val, preferred_element_type=jnp.float32)
    return result.astype(jnp.bfloat16).reshape(seq_len, -1)


def gathered_plan(hidden_in, norm_gain, q_weight, k_weight, v_weight):
    tensor_count = lax.axis_size("tensor")
    whole_rows, whole_gain = (
        lax.all_gather(hidden_in, "tensor", axis=1, tiled=True),
        lax.all_gather(norm_gain, "tensor", axis=0, tiled=True),
    )
    values = whole_rows.astype(jnp.float32)
    meansq = jnp.mean(values * values, axis=-1, keepdims=True)
    normed = (values * lax.rsqrt(meansq + 1e-05) * whole_gain.astype(jnp.float32)).astype(
        jnp.bfloat16
    )
    own_rows = q_weight.shape[0]
    kv_heads = k_weight.shape[1] // HD
    repeat_count = tensor_count // kv_heads
    q_send = q_weight.reshape(own_rows, tensor_count, -1)
    k_send = jnp.repeat(k_weight.reshape(own_rows, kv_heads, HD), repeat_count, axis=1)
    v_send = jnp.repeat(v_weight.reshape(own_rows, kv_heads, HD), repeat_count, axis=1)
    sends = jnp.concatenate([k_send, v_send, q_send], axis=2)
    recv = lax.all_to_all(sends, "tensor", split_axis=1, concat_axis=0, tiled=True)
    full = lax.all_gather(recv.reshape(-1, recv.shape[2]), "batch", axis=0, tiled=True)
    lin = jnp.dot(normed, full, preferred_element_type=jnp.float32)
    tables = rotary_tables(normed.shape[0], HD)
    k_rot = rotate_heads(lin[:, :HD], tables)[:, 0, :]
    v_val = lin[:, HD : 2 * HD].astype(jnp.bfloat16)
    return attend(rotate_heads(lin[:, 2 * HD :], tables), k_rot, v_val)


def move(value, route):
    pairs = []
    for flat in range(32):
        to = route(flat >> 3, flat >> 2 & 1, flat >> 1 & 1, flat & 1)
        if to is not None:
            pairs.append((flat, ((to[0] * 2 + to[1]) * 2 + to[2]) * 2 + to[3]))
    return lax.ppermute(value, AXES, pairs)


def swap_x(z, x, y, c):
    return z, 1 - x, y, c


def swap_y(z, x, y, c):
    return z, x, 1 - y, c


def swap_xy(z, x, y, c):
    return z, 1 - x, 1 - y, c


def swap_c(z, x, y, c):
    return z, x, y, 1 - c


def swap_near(z, x, y, c):
    return z ^ 1, x, y, c


def swap_far(z, x, y, c):
    return z ^ 2, x, y, c


CHUNKS = ((0, 2), (2, 5), (5, 8), (8, 10))
VMEM = 16 * 2**20


def place():
    batch, tensor = lax.axis_index("batch"), lax.axis_index("tensor")
    return batch >> 1, batch & 1, tensor >> 1, tensor & 1


def pick(pair, index):
    return lax.dynamic_index_in_dim(pair, index, 0, keepdims=False)


def call(kernel, out_shape, scratch=(), flops=0, name=None):
    shapes = out_shape if isinstance(out_shape, (list, tuple)) else (out_shape,)
    size = sum(2 * s.size * s.dtype.itemsize for s in shapes)
    return pl.pallas_call(
        kernel,
        out_shape=out_shape,
        scratch_shapes=scratch,
        compiler_params=pltpu.CompilerParams(vmem_limit_bytes=VMEM),
        cost_estimate=pl.CostEstimate(flops=flops, bytes_accessed=size, transcendentals=0),
        name=name,
    )


def pack_kernel(q_ref, k_ref, v_ref, *outs):
    _, x, y, _ = place()
    q_cols = outs[0].shape[1] - 2 * HD
    for out, px, py in zip(outs, (x, 1 - x, x, 1 - x), (y, y, 1 - y, 1 - y)):
        group = 2 * py + px
        out[:, :HD] = k_ref[:, pl.ds(pl.multiple_of(group * HD, HD), HD)]
        out[:, HD : 2 * HD] = v_ref[:, pl.ds(pl.multiple_of(group * HD, HD), HD)]
        out[:, 2 * HD :] = q_ref[:, pl.ds(pl.multiple_of(group * q_cols, HD), q_cols)]


def rest_kernel(own_ref, a_ref, b_ref, c_ref, far_ref, all_ref, *outs):
    own = a_ref.shape[0]
    for i, ref in enumerate((own_ref, a_ref, b_ref, c_ref, far_ref)):
        all_ref[i * own : (i + 1) * own, :] = ref[...]
        for out, (lo, hi) in zip(outs, CHUNKS):
            if 0 < i < 4:
                out[(i - 1) * own : i * own, :] = ref[:, lo * HD : hi * HD]


def squares_kernel(rows_ref, out):
    value = rows_ref[...].astype(jnp.float32)
    total = jnp.sum(value * value, axis=1, keepdims=True)
    out[...] = jnp.transpose(jnp.broadcast_to(total, (total.shape[0], HD)))[: out.shape[0], :]


def stamp_kernel(rows_ref, gain_ref, own_ref, got_ref, out):
    rows, feats = rows_ref.shape
    out[:rows, :] = rows_ref[...]
    left = own_ref[...] + got_ref[...]
    parts = []
    for _ in range(3):
        part = left.astype(jnp.bfloat16).astype(jnp.float32)
        parts.append(part)
        left = left - part
    parts.append(jnp.zeros((left.shape[0], feats - 3 * rows), jnp.float32))
    tile = jnp.concatenate(parts, axis=1)
    at = lax.broadcasted_iota(jnp.int32, tile.shape, 0)
    tile = jnp.where(at == 0, gain_ref[...].astype(jnp.float32), tile)
    out[rows:, :] = jnp.concatenate([tile, tile], axis=0).astype(jnp.bfloat16)


def scale_kernel(here, by_x, by_y, by_xy, out):
    z, x, y, c = place()
    rows, feats = out.shape[0], here.shape[1]
    own = feats // 8
    near = y == z >> 1

    def fill(same, other):
        tiles = [ref[rows:, :].astype(jnp.float32) for ref in (same, other)]
        total = sum(tile[1:2, i * rows : (i + 1) * rows] for tile in tiles for i in range(3))
        scale = lax.rsqrt(total / (4 * feats) + 1e-05)
        scale = jnp.transpose(jnp.broadcast_to(scale, (HD, rows)))[:, :1]
        for ref, tile, is_near in ((same, tiles[0], near), (other, tiles[1], jnp.logical_not(near))):
            value = ref[:rows, :].astype(jnp.float32) * scale * tile[:1, :]
            value = value.astype(jnp.bfloat16)
            for i in range(8):
                core = (i & 1) ^ c
                piece = (i >> 2 ^ x) + 2 * (i >> 1 & 1 ^ y)
                at_far = jnp.where(piece == 0, 5 * core + 4, 9 + 3 * core + piece)
                at = jnp.where(is_near, 5 * core + piece, at_far)
                out[:, pl.ds(pl.multiple_of(at * own, own), own)] = value[:, i * own : (i + 1) * own]

    @pl.when(c == x)
    def _():
        fill(here, by_y)

    @pl.when(c != x)
    def _():
        fill(by_x, by_xy)


def dot(a, b):
    return jnp.dot(a, b, preferred_element_type=jnp.float32)


def early_kernel(lhs, mine, other, out):
    depth = mine.shape[0]
    out[...] = dot(lhs[:, :depth], mine[...]) + dot(lhs[:, depth : 2 * depth], other[...])


def late_kernel(lo, hi, lhs, early, rest, rest_core, out):
    depth = rest.shape[0]
    start = lhs.shape[1] - 2 * depth
    got = dot(lhs[:, start : start + depth], rest[...]) + dot(lhs[:, start + depth :], rest_core[...])
    out[...] = got + early[:, lo * HD : hi * HD]


def turn(value, cosine, sine):
    return (value * cosine + pltpu.roll(value, HD // 2, 1) * sine).astype(jnp.bfloat16)


def keys_kernel(near_ref, got_ref, cos_ref, sin_ref, k_ref, v_ref):
    lin = near_ref[...] + got_ref[...]
    k_ref[...] = turn(lin[:, :HD], cos_ref[...], sin_ref[...])
    v_ref[...] = lin[:, HD:].astype(jnp.bfloat16)


def attend_kernel(near_ref, got_ref, cos_ref, sin_ref, k_ref, v_ref, out_ref):
    rows = near_ref.shape[0]
    cosine, sine = cos_ref[...], sin_ref[...]
    half = rows // 2
    scale = 1.0 / (HD**0.5)
    above = lax.broadcasted_iota(jnp.int32, (half, half), 1) > lax.broadcasted_iota(
        jnp.int32, (half, half), 0
    )
    for h in range(out_ref.shape[1] // HD):
        span = slice(h * HD, (h + 1) * HD)
        q = turn(near_ref[:, span] + got_ref[:, span], cosine, sine)
        for block in range(2):
            mine = q[block * half : (block + 1) * half]
            parts = []
            for other in range(block + 1):
                keys = k_ref[other * half : (other + 1) * half, :]
                s = lax.dot_general(
                    mine, keys, (((1,), (1,)), ((), ())), preferred_element_type=jnp.float32
                )
                s = s * scale
                parts.append(jnp.where(above, -1e30, s) if other == block else s)
            s = parts[0] if block == 0 else jnp.concatenate(parts, axis=1)
            expo = jnp.exp(s - jnp.max(s, axis=1, keepdims=True))
            probs = (expo / jnp.sum(expo, axis=1, keepdims=True)).astype(jnp.bfloat16)
            got = jnp.dot(
                probs, v_ref[: (block + 1) * half, :], preferred_element_type=jnp.float32
            )
            out_ref[block * half : (block + 1) * half, span] = got.astype(
                jnp.bfloat16
            )


def split_plan(hidden_in, norm_gain, q_weight, k_weight, v_weight):
    z, x, y, c = place()
    home = c == z & 1
    direct = c == x
    rows, feats = hidden_in.shape
    own = q_weight.shape[0]
    cols = (q_weight.shape[1] + k_weight.shape[1] + v_weight.shape[1]) // 4
    bf16 = jnp.bfloat16

    mine, for_x, for_y, for_xy = call(
        pack_kernel, [jax.ShapeDtypeStruct((own, cols), bf16)] * 4, name="pack"
    )(q_weight, k_weight, v_weight)
    def to_other_plane(z, x, y, c):
        return None if c == z & 1 else (z ^ 1, x, y, x)

    def to_core(z, x, y, c):
        return (z, x, y, x) if c == z & 1 and c != x else None

    squares = call(squares_kernel, jax.ShapeDtypeStruct((8, rows), jnp.float32), name="squares")(
        hidden_in
    )
    stamped = call(stamp_kernel, jax.ShapeDtypeStruct((rows + 16, feats), bf16), name="stamp")(
        hidden_in, norm_gain[None, :], squares, move(squares, swap_c)
    )
    here_far = move(stamped, to_other_plane)
    here_near = move(stamped, to_core)
    for_xy, here_near = lax.optimization_barrier((for_xy, here_near))
    here_near = jnp.where(home, stamped, here_near)
    far_mine = move(mine, swap_far)
    pieces = (move(for_x, swap_x), move(for_y, swap_y), move(for_xy, swap_xy))
    mine, far_mine, pieces, here_near = lax.optimization_barrier(
        (mine, far_mine, pieces, here_near)
    )

    widths = [(hi - lo) * HD for lo, hi in CHUNKS]
    mine_all, *rest = call(
        rest_kernel,
        [jax.ShapeDtypeStruct((5 * own, cols), bf16)]
        + [jax.ShapeDtypeStruct((3 * own, n), bf16) for n in widths],
        name="rest",
    )(mine, *pieces, far_mine)

    def give(dx, dy):
        return lambda z, x, y, c: (z, x ^ dx, y ^ dy, c) if c == x else None

    def spread(block):
        return (block, move(block, give(1, 0)), move(block, give(0, 1)), move(block, give(1, 1)))

    def normed(blocks):
        shape = jax.ShapeDtypeStruct((rows, 2 * feats), bf16)
        return call(scale_kernel, shape, name="scale_rows")(*blocks)

    far_rest = [move(rest[0], swap_far)]
    rest[1], far_rest[0] = lax.optimization_barrier((rest[1], far_rest[0]))
    far_rest.append(move(rest[1], swap_far))
    far_rows = spread(here_far)
    other_all = move(mine_all, swap_c)

    far_rows, here_near, other_all, far_rest[0], far_rest[1], rest[2] = lax.optimization_barrier(
        (far_rows, here_near, other_all, far_rest[0], far_rest[1], rest[2])
    )
    far_rest.append(move(rest[2], swap_far))
    near_rows = spread(here_near)

    def start(blocks):
        block = normed(blocks)
        shape = jax.ShapeDtypeStruct((rows, cols), jnp.float32)
        return block, call(early_kernel, shape, name="early")(block, mine_all, other_all)

    def finish(block, early, j):
        shape = jax.ShapeDtypeStruct((rows, widths[j]), jnp.float32)
        return call(lambda *refs: late_kernel(*CHUNKS[j], *refs), shape, name="late")(
            block, early, far_rest[j], rest_core[j]
        )

    def exchange(j):
        part = finish(*far_part, j)
        if j == 0:
            return move(part, swap_near)
        return move(part.astype(jnp.float16), swap_near).astype(jnp.float32)

    rest_core = [move(part, swap_c) for part in far_rest[:2]]
    far_part = start(far_rows)
    first = finish(*far_part, 1)
    rest[3], far_rest[2], first = lax.optimization_barrier((rest[3], far_rest[2], first))
    far_rest.append(move(rest[3], swap_far))
    rest_core += [move(part, swap_c) for part in far_rest[2:]]
    sums = [exchange(0), move(first.astype(jnp.float16), swap_near).astype(jnp.float32)]
    sums += [exchange(2), exchange(3)]

    cosine, sine = rotary_tables(rows, HD)
    cosine = jnp.concatenate([cosine, cosine], axis=1)
    sine = jnp.concatenate([-sine, sine], axis=1)

    def to_owner(z, x, y, c):
        return None if x == c else (z, c, y, x)

    near_part = start(near_rows)
    results = []
    k_rot, v_val = call(
        keys_kernel, [jax.ShapeDtypeStruct((rows, HD), bf16)] * 2, name="keys"
    )(finish(*near_part, 0), sums[0], cosine, sine)
    for j in range(1, len(CHUNKS)):
        out = call(attend_kernel, jax.ShapeDtypeStruct((rows, widths[j]), bf16), name="attend")(
            finish(*near_part, j), sums[j], cosine, sine, k_rot, v_val
        )
        results.append(jnp.where(direct, out, move(out, to_owner)))
    return jnp.concatenate(results, axis=1)


def solution(mesh):
    placed = (
        P("batch", "tensor"),
        P("tensor"),
        P(("batch", "tensor"), None),
        P(("batch", "tensor"), None),
        P(("batch", "tensor"), None),
    )
    plan = split_plan if dict(mesh.shape) == {"batch": 8, "tensor": 4} else gathered_plan
    return jax.shard_map(
        plan, mesh=mesh, in_specs=placed, out_specs=P("batch", "tensor"), check_vma=False
    )
```

```python
import jax
import jax.numpy as jnp
from jax import lax
from jax.experimental import pallas as pl
from jax.experimental.pallas import tpu as pltpu
from jax.sharding import PartitionSpec as P

HD = 128
AXES = ("batch", "tensor")


def rotary_tables(seq_len, head_size):
    half = head_size // 2
    position = jnp.arange(seq_len, dtype=jnp.float32)
    freqs = 500000.0 ** (-(jnp.arange(half, dtype=jnp.float32) * 2.0) / head_size)
    angles = position[:, None] * freqs[None, :]
    return jnp.cos(angles), jnp.sin(angles)


def rotate_heads(field, tables):
    seq_len = field.shape[0]
    shaped = field.reshape(seq_len, -1, HD)
    half = HD // 2
    cosine = tables[0][:, None, :]
    sine = tables[1][:, None, :]
    first = shaped[..., :half]
    second = shaped[..., half:]
    turned = jnp.concatenate(
        [first * cosine - second * sine, second * cosine + first * sine], axis=-1
    )
    return turned.astype(jnp.bfloat16)


def attend(q_rot, k_rot, v_val):
    seq_len = q_rot.shape[0]
    scores = jnp.einsum("shd,td->hst", q_rot, k_rot, preferred_element_type=jnp.float32) / jnp.sqrt(
        jnp.float32(HD)
    )
    causal = jnp.tril(jnp.ones((seq_len, seq_len), dtype=bool))
    scores = jnp.where(causal[None], scores, jnp.float32(-1e30))
    top = jnp.max(scores, axis=-1, keepdims=True)
    expo = jnp.exp(scores - top)
    probs = (expo / jnp.sum(expo, axis=-1, keepdims=True)).astype(jnp.bfloat16)
    result = jnp.einsum("hst,td->shd", probs, v_val, preferred_element_type=jnp.float32)
    return result.astype(jnp.bfloat16).reshape(seq_len, -1)


def gathered_plan(hidden_in, norm_gain, q_weight, k_weight, v_weight):
    tensor_count = lax.axis_size("tensor")
    whole_rows, whole_gain = (
        lax.all_gather(hidden_in, "tensor", axis=1, tiled=True),
        lax.all_gather(norm_gain, "tensor", axis=0, tiled=True),
    )
    values = whole_rows.astype(jnp.float32)
    meansq = jnp.mean(values * values, axis=-1, keepdims=True)
    normed = (values * lax.rsqrt(meansq + 1e-05) * whole_gain.astype(jnp.float32)).astype(
        jnp.bfloat16
    )
    own_rows = q_weight.shape[0]
    kv_heads = k_weight.shape[1] // HD
    repeat_count = tensor_count // kv_heads
    q_send = q_weight.reshape(own_rows, tensor_count, -1)
    k_send = jnp.repeat(k_weight.reshape(own_rows, kv_heads, HD), repeat_count, axis=1)
    v_send = jnp.repeat(v_weight.reshape(own_rows, kv_heads, HD), repeat_count, axis=1)
    sends = jnp.concatenate([k_send, v_send, q_send], axis=2)
    recv = lax.all_to_all(sends, "tensor", split_axis=1, concat_axis=0, tiled=True)
    full = lax.all_gather(recv.reshape(-1, recv.shape[2]), "batch", axis=0, tiled=True)
    lin = jnp.dot(normed, full, preferred_element_type=jnp.float32)
    tables = rotary_tables(normed.shape[0], HD)
    k_rot = rotate_heads(lin[:, :HD], tables)[:, 0, :]
    v_val = lin[:, HD : 2 * HD].astype(jnp.bfloat16)
    return attend(rotate_heads(lin[:, 2 * HD :], tables), k_rot, v_val)


def move(value, route):
    pairs = []
    for flat in range(32):
        to = route(flat >> 3, flat >> 2 & 1, flat >> 1 & 1, flat & 1)
        if to is not None:
            pairs.append((flat, ((to[0] * 2 + to[1]) * 2 + to[2]) * 2 + to[3]))
    return lax.ppermute(value, AXES, pairs)


def swap_x(z, x, y, c):
    return z, 1 - x, y, c


def swap_y(z, x, y, c):
    return z, x, 1 - y, c


def swap_xy(z, x, y, c):
    return z, 1 - x, 1 - y, c


def swap_c(z, x, y, c):
    return z, x, y, 1 - c


def swap_near(z, x, y, c):
    return z ^ 1, x, y, c


def swap_far(z, x, y, c):
    return z ^ 2, x, y, c


CHUNKS = ((0, 3), (3, 5), (5, 8), (8, 10))
PARTS = (
    ((0, 1), ((1, 0), (1, 1), (0, 0), (0, 1), (0, 2))),
    ((2,), ((0, 0), (0, 1), (0, 2))),
    ((3,), ((0, 0), (0, 1))),
)
VMEM = {
    "pack": 8, "squares": 6, "stamp": 6, "rest": 10, "scale_rows": 16, "early": 15,
    "late": 14, "whole": 18, "keys": 4, "attend": 6, "place": 5,
}


def place():
    batch, tensor = lax.axis_index("batch"), lax.axis_index("tensor")
    return batch >> 1, batch & 1, tensor >> 1, tensor & 1


def pick(pair, index):
    return lax.dynamic_index_in_dim(pair, index, 0, keepdims=False)


def call(kernel, out_shape, name=None, flops=0):
    shapes = out_shape if isinstance(out_shape, (list, tuple)) else (out_shape,)
    size = sum(2 * s.size * s.dtype.itemsize for s in shapes)
    return pl.pallas_call(
        kernel,
        out_shape=out_shape,
        compiler_params=pltpu.CompilerParams(vmem_limit_bytes=VMEM[name] * 2**20),
        cost_estimate=pl.CostEstimate(flops=flops, bytes_accessed=size, transcendentals=0),
        name=name,
    )


def pack_kernel(q_ref, k_ref, v_ref, *outs):
    _, x, y, _ = place()
    q_cols = outs[0].shape[1] - 2 * HD
    for out, px, py in zip(outs, (x, 1 - x, x, 1 - x), (y, y, 1 - y, 1 - y)):
        group = 2 * py + px
        out[:, :HD] = k_ref[:, pl.ds(pl.multiple_of(group * HD, HD), HD)]
        out[:, HD : 2 * HD] = v_ref[:, pl.ds(pl.multiple_of(group * HD, HD), HD)]
        out[:, 2 * HD :] = q_ref[:, pl.ds(pl.multiple_of(group * q_cols, HD), q_cols)]


def rest_kernel(own_ref, a_ref, b_ref, c_ref, far_ref, all_ref, *outs):
    own = a_ref.shape[0]
    for i, ref in enumerate((own_ref, a_ref, b_ref, c_ref, far_ref)):
        all_ref[i * own : (i + 1) * own, :] = ref[...]
        for out, (lo, hi) in zip(outs, CHUNKS):
            if 0 < i < 4:
                out[(i - 1) * own : i * own, :] = ref[:, lo * HD : hi * HD]


def squares_kernel(rows_ref, out):
    value = rows_ref[...].astype(jnp.float32)
    total = jnp.sum(value * value, axis=1, keepdims=True)
    out[...] = jnp.transpose(jnp.broadcast_to(total, (total.shape[0], HD)))[: out.shape[0], :]


def stamp_kernel(rows_ref, gain_ref, own_ref, got_ref, out):
    rows, feats = rows_ref.shape
    out[:rows, :] = rows_ref[...]
    left = own_ref[...] + got_ref[...]
    parts = []
    for _ in range(3):
        part = left.astype(jnp.bfloat16).astype(jnp.float32)
        parts.append(part)
        left = left - part
    parts.append(jnp.zeros((left.shape[0], feats - 3 * rows), jnp.float32))
    tile = jnp.concatenate(parts, axis=1)
    at = lax.broadcasted_iota(jnp.int32, tile.shape, 0)
    tile = jnp.where(at == 0, gain_ref[...].astype(jnp.float32), tile)
    out[rows:, :] = jnp.concatenate([tile, tile], axis=0).astype(jnp.bfloat16)


def scale_kernel(here, by_x, by_y, by_xy, *refs):
    z, x, y, c = place()
    out = refs[-1]
    rows, feats = out.shape[0], here.shape[1]
    own = feats // 8
    near = y == z >> 1
    home = jnp.logical_and(len(refs) > 1, c == z & 1)
    kept = refs[0] if len(refs) > 1 else here

    def fill(same, other):
        tiles = [ref[rows:, :].astype(jnp.float32) for ref in (same, other)]
        total = sum(tile[1:2, i * rows : (i + 1) * rows] for tile in tiles for i in range(3))
        scale = lax.rsqrt(total / (4 * feats) + 1e-05)
        scale = jnp.transpose(jnp.broadcast_to(scale, (HD, rows)))[:, :1]
        for ref, tile, is_near in (
            (same, tiles[0], near), (other, tiles[1], jnp.logical_not(near))
        ):
            for i in range(8):
                span = slice(i * own, (i + 1) * own)
                core = (i & 1) ^ c
                piece = (i >> 2 ^ x) + 2 * (i >> 1 & 1 ^ y)
                at_far = jnp.where(piece == 0, 5 * core + 4, 9 + 3 * core + piece)
                at = jnp.where(is_near, 5 * core + piece, at_far)
                to = pl.ds(pl.multiple_of(at * own, own), own)
                value = ref[:rows, span].astype(jnp.float32) * scale * tile[:1, span]
                out[:, to] = value.astype(jnp.bfloat16)

    @pl.when(jnp.logical_and(c == x, jnp.logical_not(home)))
    def _():
        fill(here, by_y)

    @pl.when(jnp.logical_and(c == x, home))
    def _():
        fill(kept, by_y)

    @pl.when(c != x)
    def _():
        fill(by_x, by_xy)


def dot(a, b):
    return jnp.dot(a, b, preferred_element_type=jnp.float32)


def early_kernel(lhs, *refs):
    total, at = 0.0, 0
    for ref in refs[:-1]:
        total = total + dot(lhs[:, at : at + ref.shape[0]], ref[...])
        at += ref.shape[0]
    refs[-1][...] = total


def late_kernel(chunks, places, lhs, early, *refs):
    count = len(chunks)
    outs = refs[2 * count :]
    places = iter(places)
    for j, rest, rest_core in zip(chunks, refs[:count], refs[count : 2 * count]):
        depth = rest.shape[0]
        start = lhs.shape[1] - 2 * depth
        lo, hi = CHUNKS[j]
        got = dot(lhs[:, start : start + depth], rest[...])
        got = got + dot(lhs[:, start + depth :], rest_core[...]) + early[:, lo * HD : hi * HD]
        for h in range(hi - lo):
            i, at = next(places)
            outs[i][:, at * HD : (at + 1) * HD] = got[:, h * HD : (h + 1) * HD]


def whole_kernel(lhs, mine, other, *refs):
    count = len(CHUNKS)
    rest, rest_core, outs = refs[:count], refs[count : 2 * count], list(refs[2 * count :])
    depth = mine.shape[0]
    for chunks, places in PARTS:
        parts = [outs.pop(0) for _ in range(1 + max(i for i, _ in places))]
        places = iter(places)
        for j in chunks:
            lo, hi = CHUNKS[j]
            span = slice(lo * HD, hi * HD)
            got, at = 0.0, 0
            for weight in (mine[:, span], other[:, span], rest[j][...], rest_core[j][...]):
                got = got + dot(lhs[:, at : at + weight.shape[0]], weight)
                at += weight.shape[0]
            for h in range(hi - lo):
                i, to = next(places)
                parts[i][:, to * HD : (to + 1) * HD] = got[:, h * HD : (h + 1) * HD]


def place_kernel(*refs):
    _, x, _, c = place()
    out = refs[-1]
    count = len(refs) // 2

    def fill(parts):
        at = 0
        for ref in parts:
            out[:, at : at + ref.shape[1]] = ref[...]
            at += ref.shape[1]

    @pl.when(c == x)
    def _():
        fill(refs[:count])

    @pl.when(c != x)
    def _():
        fill(refs[count:-1])


def turn(value, cosine, sine):
    return (value * cosine + pltpu.roll(value, HD // 2, 1) * sine).astype(jnp.bfloat16)


def keys_kernel(near_ref, got_ref, cos_ref, sin_ref, k_ref, v_ref):
    lin = near_ref[...] + got_ref[...]
    k_ref[...] = turn(lin[:, :HD], cos_ref[...], sin_ref[...])
    v_ref[...] = lin[:, HD:].astype(jnp.bfloat16)


def attend_kernel(near_ref, got_ref, cos_ref, sin_ref, k_ref, v_ref, out_ref):
    rows = near_ref.shape[0]
    cosine, sine = cos_ref[...], sin_ref[...]
    half = rows // 2
    scale = 1.0 / (HD**0.5)
    above = lax.broadcasted_iota(jnp.int32, (half, half), 1) > lax.broadcasted_iota(
        jnp.int32, (half, half), 0
    )
    for h in range(out_ref.shape[1] // HD):
        span = slice(h * HD, (h + 1) * HD)
        q = turn(near_ref[:, span] + got_ref[:, span], cosine, sine)
        for block in range(2):
            mine = q[block * half : (block + 1) * half]
            parts = []
            for other in range(block + 1):
                keys = k_ref[other * half : (other + 1) * half, :]
                s = lax.dot_general(
                    mine, keys, (((1,), (1,)), ((), ())), preferred_element_type=jnp.float32
                )
                s = s * scale
                parts.append(jnp.where(above, -1e30, s) if other == block else s)
            s = parts[0] if block == 0 else jnp.concatenate(parts, axis=1)
            expo = jnp.exp(s - jnp.max(s, axis=1, keepdims=True))
            probs = (expo / jnp.sum(expo, axis=1, keepdims=True)).astype(jnp.bfloat16)
            got = jnp.dot(
                probs, v_ref[: (block + 1) * half, :], preferred_element_type=jnp.float32
            )
            out_ref[block * half : (block + 1) * half, span] = got.astype(
                jnp.bfloat16
            )


def split_plan(hidden_in, norm_gain, q_weight, k_weight, v_weight):
    z, x, y, c = place()
    home = c == z & 1
    direct = c == x
    rows, feats = hidden_in.shape
    own = q_weight.shape[0]
    cols = (q_weight.shape[1] + k_weight.shape[1] + v_weight.shape[1]) // 4
    bf16 = jnp.bfloat16

    mine, for_x, for_y, for_xy = call(
        pack_kernel, [jax.ShapeDtypeStruct((own, cols), bf16)] * 4, name="pack"
    )(q_weight, k_weight, v_weight)
    def to_other_plane(z, x, y, c):
        return None if c == z & 1 else (z ^ 1, x, y, x)

    def to_core(z, x, y, c):
        return (z, x, y, x) if c == z & 1 and c != x else None

    squares = call(squares_kernel, jax.ShapeDtypeStruct((8, rows), jnp.float32), name="squares")(
        hidden_in
    )
    stamped = call(stamp_kernel, jax.ShapeDtypeStruct((rows + 16, feats), bf16), name="stamp")(
        hidden_in, norm_gain[None, :], squares, move(squares, swap_c)
    )
    here_far = move(stamped, to_other_plane)
    far_mine = move(mine, swap_far)
    pieces = (move(for_x, swap_x), move(for_y, swap_y), move(for_xy, swap_xy))
    mine, far_mine, pieces = lax.optimization_barrier((mine, far_mine, pieces))
    mine_all, *rest = call(
        rest_kernel,
        [jax.ShapeDtypeStruct((5 * own, cols), bf16)]
        + [jax.ShapeDtypeStruct((3 * own, (hi - lo) * HD), bf16) for lo, hi in CHUNKS],
        name="rest",
    )(mine, *pieces, far_mine)

    def give_far(dx, dy):
        return lambda z, x, y, c: (z, x ^ dx, y ^ dy, c) if c == x else None

    def give_near(dx, dy):
        return lambda z, x, y, c: (z, x ^ dx, y ^ dy, x) if c == z & 1 else None

    def spread(block, give):
        return [move(block, give(1, 0)), move(block, give(0, 1)), move(block, give(1, 1))]

    def normed(blocks):
        shape = jax.ShapeDtypeStruct((rows, 2 * feats), bf16)
        return call(scale_kernel, shape, name="scale_rows", flops=2 * 10**10)(*blocks)

    here_far, rest, mine_all = lax.optimization_barrier((here_far, rest, mine_all))
    far_rows = [here_far, *spread(here_far, give_far)]
    far_rest = [move(rest[0], swap_far)]
    rest[1], far_rest[0] = lax.optimization_barrier((rest[1], far_rest[0]))
    far_rest.append(move(rest[1], swap_far))
    cosine, sine = rotary_tables(rows, HD)
    cosine = jnp.concatenate([cosine, cosine], axis=1)
    sine = jnp.concatenate([-sine, sine], axis=1)
    other_all, here_near = move(mine_all, swap_c), move(stamped, to_core)
    rest_core = [move(far_rest[0], swap_c)]
    far_block = normed(far_rows)
    far_block, far_rest, rest_core, stamped, here_near, other_all, rest[2], cosine, sine = (
        lax.optimization_barrier(
            (far_block, far_rest, rest_core, stamped, here_near, other_all, rest[2], cosine, sine)
        )
    )

    near_rows = spread(stamped, give_near)
    far_rest.append(move(rest[2], swap_far))
    rest_core.append(move(far_rest[1], swap_c))
    rest[3], far_rest[2] = lax.optimization_barrier((rest[3], far_rest[2]))
    far_rest.append(move(rest[3], swap_far))
    rest_core.append(move(far_rest[2], swap_c))

    def start(block):
        shape = jax.ShapeDtypeStruct((rows, cols), jnp.float32)
        return block, call(early_kernel, shape, name="early")(block, mine_all, other_all)

    def finish(block, early, i):
        chunks, places = PARTS[i]
        widths = [HD * sum(out == j for out, _ in places) for j in range(2)]
        shapes = [jax.ShapeDtypeStruct((rows, n), jnp.float32) for n in widths if n > 0]
        return call(lambda *refs: late_kernel(chunks, places, *refs), shapes, name="late")(
            block, early, *[far_rest[j] for j in chunks], *[rest_core[j] for j in chunks]
        )

    def send(part):
        return move(part.astype(jnp.float16), swap_near)

    far_part = start(far_block)
    part, kv_part = finish(*far_part, 0)
    kv_sum, sums = move(kv_part, swap_near), [send(part)]
    near_block = normed((here_near, *near_rows, stamped))
    near_block, far_rest, rest_core, kv_sum, sums = lax.optimization_barrier(
        (near_block, far_rest, rest_core, kv_sum, sums)
    )
    sums.append(send(finish(*far_part, 1)[0]))
    rest_core.append(move(far_rest[3], swap_c))
    part = finish(*far_part, 2)[0]
    sums.append(send(part))
    near_block, part = lax.optimization_barrier((near_block, part))

    def to_owner(z, x, y, c):
        return None if x == c else (z, c, y, x)

    widths = [[HD * sum(i == j for i, _ in places) for j in range(2)] for _, places in PARTS]
    part, kv_part, *parts = call(
        whole_kernel,
        [jax.ShapeDtypeStruct((rows, n), jnp.float32) for ns in widths for n in ns if n > 0],
        name="whole",
    )(near_block, mine_all, other_all, *far_rest, *rest_core)
    parts = [part, *parts]
    k_rot, v_val = call(
        keys_kernel, [jax.ShapeDtypeStruct((rows, HD), bf16)] * 2, name="keys"
    )(kv_part, kv_sum, cosine, sine)
    outs = [
        call(attend_kernel, jax.ShapeDtypeStruct(part.shape, bf16), name="attend")(
            part, got.astype(jnp.float32), cosine, sine, k_rot, v_val
        )
        for part, got in zip(parts, sums)
    ]
    came = [move(out, to_owner) for out in outs]
    return call(place_kernel, jax.ShapeDtypeStruct((rows, q_weight.shape[1] // 4), bf16), name="place")(
        *outs, *came
    )


def solution(mesh):
    placed = (
        P("batch", "tensor"),
        P("tensor"),
        P(("batch", "tensor"), None),
        P(("batch", "tensor"), None),
        P(("batch", "tensor"), None),
    )
    plan = split_plan if dict(mesh.shape) == {"batch": 8, "tensor": 4} else gathered_plan
    return jax.shard_map(
        plan, mesh=mesh, in_specs=placed, out_specs=P("batch", "tensor"), check_vma=False
    )
```

```python
import jax
import jax.numpy as jnp
from jax import lax
from jax.experimental import pallas as pl
from jax.experimental.pallas import tpu as pltpu
from jax.sharding import PartitionSpec as P

HD = 128
AXES = ("batch", "tensor")


def rotary_tables(seq_len, head_size):
    half = head_size // 2
    position = jnp.arange(seq_len, dtype=jnp.float32)
    freqs = 500000.0 ** (-(jnp.arange(half, dtype=jnp.float32) * 2.0) / head_size)
    angles = position[:, None] * freqs[None, :]
    return jnp.cos(angles), jnp.sin(angles)


def rotate_heads(field, tables):
    seq_len = field.shape[0]
    shaped = field.reshape(seq_len, -1, HD)
    half = HD // 2
    cosine = tables[0][:, None, :]
    sine = tables[1][:, None, :]
    first = shaped[..., :half]
    second = shaped[..., half:]
    turned = jnp.concatenate(
        [first * cosine - second * sine, second * cosine + first * sine], axis=-1
    )
    return turned.astype(jnp.bfloat16)


def attend(q_rot, k_rot, v_val):
    seq_len = q_rot.shape[0]
    scores = jnp.einsum("shd,td->hst", q_rot, k_rot, preferred_element_type=jnp.float32) / jnp.sqrt(
        jnp.float32(HD)
    )
    causal = jnp.tril(jnp.ones((seq_len, seq_len), dtype=bool))
    scores = jnp.where(causal[None], scores, jnp.float32(-1e30))
    top = jnp.max(scores, axis=-1, keepdims=True)
    expo = jnp.exp(scores - top)
    probs = (expo / jnp.sum(expo, axis=-1, keepdims=True)).astype(jnp.bfloat16)
    result = jnp.einsum("hst,td->shd", probs, v_val, preferred_element_type=jnp.float32)
    return result.astype(jnp.bfloat16).reshape(seq_len, -1)


def gathered_plan(hidden_in, norm_gain, q_weight, k_weight, v_weight):
    tensor_count = lax.axis_size("tensor")
    whole_rows, whole_gain = (
        lax.all_gather(hidden_in, "tensor", axis=1, tiled=True),
        lax.all_gather(norm_gain, "tensor", axis=0, tiled=True),
    )
    values = whole_rows.astype(jnp.float32)
    meansq = jnp.mean(values * values, axis=-1, keepdims=True)
    normed = (values * lax.rsqrt(meansq + 1e-05) * whole_gain.astype(jnp.float32)).astype(
        jnp.bfloat16
    )
    own_rows = q_weight.shape[0]
    kv_heads = k_weight.shape[1] // HD
    repeat_count = tensor_count // kv_heads
    q_send = q_weight.reshape(own_rows, tensor_count, -1)
    k_send = jnp.repeat(k_weight.reshape(own_rows, kv_heads, HD), repeat_count, axis=1)
    v_send = jnp.repeat(v_weight.reshape(own_rows, kv_heads, HD), repeat_count, axis=1)
    sends = jnp.concatenate([k_send, v_send, q_send], axis=2)
    recv = lax.all_to_all(sends, "tensor", split_axis=1, concat_axis=0, tiled=True)
    full = lax.all_gather(recv.reshape(-1, recv.shape[2]), "batch", axis=0, tiled=True)
    lin = jnp.dot(normed, full, preferred_element_type=jnp.float32)
    tables = rotary_tables(normed.shape[0], HD)
    k_rot = rotate_heads(lin[:, :HD], tables)[:, 0, :]
    v_val = lin[:, HD : 2 * HD].astype(jnp.bfloat16)
    return attend(rotate_heads(lin[:, 2 * HD :], tables), k_rot, v_val)


def move(value, route):
    pairs = []
    for flat in range(32):
        to = route(flat >> 3, flat >> 2 & 1, flat >> 1 & 1, flat & 1)
        if to is not None:
            pairs.append((flat, ((to[0] * 2 + to[1]) * 2 + to[2]) * 2 + to[3]))
    return lax.ppermute(value, AXES, pairs)


def swap_x(z, x, y, c):
    return z, 1 - x, y, c


def swap_y(z, x, y, c):
    return z, x, 1 - y, c


def swap_xy(z, x, y, c):
    return z, 1 - x, 1 - y, c


def swap_c(z, x, y, c):
    return z, x, y, 1 - c


def swap_near(z, x, y, c):
    return z ^ 1, x, y, c


def swap_far(z, x, y, c):
    return z ^ 2, x, y, c


CHUNKS = ((0, 3), (3, 5), (5, 8), (8, 10))
PARTS = (
    ((0, 1), ((1, 0), (1, 1), (0, 0), (0, 1), (0, 2))),
    ((2,), ((0, 0), (0, 1), (0, 2))),
    ((3,), ((0, 0), (0, 1))),
)
VMEM = {
    "pack": 8, "squares": 6, "stamp": 6, "rest": 10, "scale_rows": 16, "early": 15,
    "late": 14, "whole": 20, "keys": 4, "attend": 10, "place": 5,
}


def place():
    batch, tensor = lax.axis_index("batch"), lax.axis_index("tensor")
    return batch >> 1, batch & 1, tensor >> 1, tensor & 1


def pick(pair, index):
    return lax.dynamic_index_in_dim(pair, index, 0, keepdims=False)


def call(kernel, out_shape, name=None, flops=0):
    shapes = out_shape if isinstance(out_shape, (list, tuple)) else (out_shape,)
    size = sum(2 * s.size * s.dtype.itemsize for s in shapes)
    return pl.pallas_call(
        kernel,
        out_shape=out_shape,
        compiler_params=pltpu.CompilerParams(vmem_limit_bytes=VMEM[name] * 2**20),
        cost_estimate=pl.CostEstimate(flops=flops, bytes_accessed=size, transcendentals=0),
        name=name,
    )


def pack_kernel(q_ref, k_ref, v_ref, *outs):
    _, x, y, _ = place()
    q_cols = outs[0].shape[1] - 2 * HD
    for out, px, py in zip(outs, (x, 1 - x, x, 1 - x), (y, y, 1 - y, 1 - y)):
        group = 2 * py + px
        out[:, :HD] = k_ref[:, pl.ds(pl.multiple_of(group * HD, HD), HD)]
        out[:, HD : 2 * HD] = v_ref[:, pl.ds(pl.multiple_of(group * HD, HD), HD)]
        out[:, 2 * HD :] = q_ref[:, pl.ds(pl.multiple_of(group * q_cols, HD), q_cols)]


def rest_kernel(own_ref, a_ref, b_ref, c_ref, far_ref, all_ref, *outs):
    own = a_ref.shape[0]
    for i, ref in enumerate((own_ref, a_ref, b_ref, c_ref, far_ref)):
        all_ref[i * own : (i + 1) * own, :] = ref[...]
        for out, (lo, hi) in zip(outs, CHUNKS):
            if 0 < i < 4:
                out[(i - 1) * own : i * own, :] = ref[:, lo * HD : hi * HD]


def squares_kernel(rows_ref, out):
    value = rows_ref[...].astype(jnp.float32)
    total = jnp.sum(value * value, axis=1, keepdims=True)
    out[...] = jnp.transpose(jnp.broadcast_to(total, (total.shape[0], HD)))[: out.shape[0], :]


def stamp_kernel(rows_ref, gain_ref, own_ref, got_ref, out):
    rows, feats = rows_ref.shape
    out[:rows, :] = rows_ref[...]
    left = own_ref[...] + got_ref[...]
    parts = []
    for _ in range(3):
        part = left.astype(jnp.bfloat16).astype(jnp.float32)
        parts.append(part)
        left = left - part
    parts.append(jnp.zeros((left.shape[0], feats - 3 * rows), jnp.float32))
    tile = jnp.concatenate(parts, axis=1)
    at = lax.broadcasted_iota(jnp.int32, tile.shape, 0)
    tile = jnp.where(at == 0, gain_ref[...].astype(jnp.float32), tile)
    out[rows:, :] = jnp.concatenate([tile, tile], axis=0).astype(jnp.bfloat16)


def scale_kernel(here, by_x, by_y, by_xy, *refs):
    z, x, y, c = place()
    out = refs[-1]
    rows, feats = out.shape[0], here.shape[1]
    own = feats // 8
    near = y == z >> 1
    home = jnp.logical_and(len(refs) > 1, c == z & 1)
    kept = refs[0] if len(refs) > 1 else here

    def fill(same, other):
        tiles = [ref[rows:, :].astype(jnp.float32) for ref in (same, other)]
        total = sum(tile[1:2, i * rows : (i + 1) * rows] for tile in tiles for i in range(3))
        scale = lax.rsqrt(total / (4 * feats) + 1e-05)
        scale = jnp.transpose(jnp.broadcast_to(scale, (HD, rows)))[:, :1]
        for ref, tile, is_near in (
            (same, tiles[0], near), (other, tiles[1], jnp.logical_not(near))
        ):
            for i in range(8):
                span = slice(i * own, (i + 1) * own)
                core = (i & 1) ^ c
                piece = (i >> 2 ^ x) + 2 * (i >> 1 & 1 ^ y)
                at_far = jnp.where(piece == 0, 5 * core + 4, 9 + 3 * core + piece)
                at = jnp.where(is_near, 5 * core + piece, at_far)
                to = pl.ds(pl.multiple_of(at * own, own), own)
                value = ref[:rows, span].astype(jnp.float32) * scale * tile[:1, span]
                out[:, to] = value.astype(jnp.bfloat16)

    @pl.when(jnp.logical_and(c == x, jnp.logical_not(home)))
    def _():
        fill(here, by_y)

    @pl.when(jnp.logical_and(c == x, home))
    def _():
        fill(kept, by_y)

    @pl.when(c != x)
    def _():
        fill(by_x, by_xy)


def dot(a, b):
    return jnp.dot(a, b, preferred_element_type=jnp.float32)


def early_kernel(lhs, *refs):
    total, at = 0.0, 0
    for ref in refs[:-1]:
        total = total + dot(lhs[:, at : at + ref.shape[0]], ref[...])
        at += ref.shape[0]
    refs[-1][...] = total


def late_kernel(chunks, places, lhs, early, *refs):
    count = len(chunks)
    outs = refs[2 * count :]
    places = iter(places)
    for j, rest, rest_core in zip(chunks, refs[:count], refs[count : 2 * count]):
        depth = rest.shape[0]
        start = lhs.shape[1] - 2 * depth
        lo, hi = CHUNKS[j]
        got = dot(lhs[:, start : start + depth], rest[...])
        got = got + dot(lhs[:, start + depth :], rest_core[...]) + early[:, lo * HD : hi * HD]
        for h in range(hi - lo):
            i, at = next(places)
            outs[i][:, at * HD : (at + 1) * HD] = got[:, h * HD : (h + 1) * HD]


def whole_kernel(lhs, mine, other, *refs):
    count = len(CHUNKS)
    rest, rest_core, outs = refs[:count], refs[count : 2 * count], list(refs[2 * count :])
    depth = mine.shape[0]
    near = dot(lhs[:, :depth], mine[...]) + dot(lhs[:, depth : 2 * depth], other[...])
    for chunks, places in PARTS:
        parts = [outs.pop(0) for _ in range(1 + max(i for i, _ in places))]
        places = iter(places)
        for j in chunks:
            lo, hi = CHUNKS[j]
            got, at = near[:, lo * HD : hi * HD], 2 * depth
            for ref in (rest[j], rest_core[j]):
                got = got + dot(lhs[:, at : at + ref.shape[0]], ref[...])
                at += ref.shape[0]
            for h in range(hi - lo):
                i, to = next(places)
                parts[i][:, to * HD : (to + 1) * HD] = got[:, h * HD : (h + 1) * HD]


def place_kernel(*refs):
    _, x, _, c = place()
    out = refs[-1]
    count = len(refs) // 2

    def fill(parts):
        at = 0
        for ref in parts:
            out[:, at : at + ref.shape[1]] = ref[...]
            at += ref.shape[1]

    @pl.when(c == x)
    def _():
        fill(refs[:count])

    @pl.when(c != x)
    def _():
        fill(refs[count:-1])


def turn(value, cosine, sine):
    return (value * cosine + pltpu.roll(value, HD // 2, 1) * sine).astype(jnp.bfloat16)


def keys_kernel(near_ref, got_ref, cos_ref, sin_ref, k_ref, v_ref):
    lin = near_ref[...] + got_ref[...]
    k_ref[...] = turn(lin[:, :HD], cos_ref[...], sin_ref[...])
    v_ref[...] = lin[:, HD:].astype(jnp.bfloat16)


def attend_kernel(near_ref, got_ref, cos_ref, sin_ref, k_ref, v_ref, out_ref):
    rows, width = out_ref.shape
    half = rows // 2
    cosine, sine = cos_ref[...], sin_ref[...]
    spans = [slice(h, h + HD) for h in range(0, width, HD)]
    queries = [turn(near_ref[:, span] + got_ref[:, span], cosine, sine) for span in spans]
    scale = 1.4426950408889634 / HD**0.5
    for lo, hi in ((0, half), (half, rows)):
        mine = jnp.concatenate([q[lo:hi] for q in queries], axis=0)
        scores = lax.dot_general(
            mine, k_ref[:hi, :], (((1,), (1,)), ((), ())), preferred_element_type=jnp.float32
        )
        row = lax.broadcasted_iota(jnp.int32, (half, hi), 0) + lo
        later = lax.broadcasted_iota(jnp.int32, (half, hi), 1) > row
        probs = []
        for h in range(len(spans)):
            s = jnp.where(later, -1e30, scores[h * half : (h + 1) * half])
            expo = jnp.exp2((s - jnp.max(s, axis=1, keepdims=True)) * scale)
            inverse = 1.0 / jnp.sum(expo, axis=1, keepdims=True)
            probs.append((expo * inverse).astype(jnp.bfloat16))
        got = dot(jnp.concatenate(probs, axis=0), v_ref[:hi, :]).astype(jnp.bfloat16)
        for h, span in enumerate(spans):
            out_ref[lo:hi, span] = got[h * half : (h + 1) * half]


def split_plan(hidden_in, norm_gain, q_weight, k_weight, v_weight):
    z, x, y, c = place()
    home = c == z & 1
    direct = c == x
    rows, feats = hidden_in.shape
    own = q_weight.shape[0]
    cols = (q_weight.shape[1] + k_weight.shape[1] + v_weight.shape[1]) // 4
    bf16 = jnp.bfloat16

    mine, for_x, for_y, for_xy = call(
        pack_kernel, [jax.ShapeDtypeStruct((own, cols), bf16)] * 4, name="pack"
    )(q_weight, k_weight, v_weight)
    def to_other_plane(z, x, y, c):
        return None if c == z & 1 else (z ^ 1, x, y, x)

    def to_core(z, x, y, c):
        return (z, x, y, x) if c == z & 1 and c != x else None

    squares = call(squares_kernel, jax.ShapeDtypeStruct((8, rows), jnp.float32), name="squares")(
        hidden_in
    )
    stamped = call(stamp_kernel, jax.ShapeDtypeStruct((rows + 16, feats), bf16), name="stamp")(
        hidden_in, norm_gain[None, :], squares, move(squares, swap_c)
    )
    here_far = move(stamped, to_other_plane)
    far_mine = move(mine, swap_far)
    pieces = (move(for_x, swap_x), move(for_y, swap_y), move(for_xy, swap_xy))
    mine, far_mine, pieces = lax.optimization_barrier((mine, far_mine, pieces))
    mine_all, *rest = call(
        rest_kernel,
        [jax.ShapeDtypeStruct((5 * own, cols), bf16)]
        + [jax.ShapeDtypeStruct((3 * own, (hi - lo) * HD), bf16) for lo, hi in CHUNKS],
        name="rest",
    )(mine, *pieces, far_mine)

    def give_far(dx, dy):
        return lambda z, x, y, c: (z, x ^ dx, y ^ dy, c) if c == x else None

    def give_near(dx, dy):
        return lambda z, x, y, c: (z, x ^ dx, y ^ dy, x) if c == z & 1 else None

    def spread(block, give):
        return [move(block, give(1, 0)), move(block, give(0, 1)), move(block, give(1, 1))]

    def normed(blocks):
        shape = jax.ShapeDtypeStruct((rows, 2 * feats), bf16)
        return call(scale_kernel, shape, name="scale_rows", flops=2 * 10**10)(*blocks)

    here_far, rest, mine_all = lax.optimization_barrier((here_far, rest, mine_all))
    far_rows = [here_far, *spread(here_far, give_far)]
    far_rest = [move(rest[0], swap_far)]
    rest[1], far_rest[0] = lax.optimization_barrier((rest[1], far_rest[0]))
    far_rest.append(move(rest[1], swap_far))
    cosine, sine = rotary_tables(rows, HD)
    cosine = jnp.concatenate([cosine, cosine], axis=1)
    sine = jnp.concatenate([-sine, sine], axis=1)
    other_all, here_near = move(mine_all, swap_c), move(stamped, to_core)
    rest_core = [move(far_rest[0], swap_c)]
    far_block = normed(far_rows)
    far_block, far_rest, rest_core, stamped, here_near, other_all, rest[2], cosine, sine = (
        lax.optimization_barrier(
            (far_block, far_rest, rest_core, stamped, here_near, other_all, rest[2], cosine, sine)
        )
    )

    near_rows = spread(stamped, give_near)
    far_rest.append(move(rest[2], swap_far))
    rest_core.append(move(far_rest[1], swap_c))
    rest[3], far_rest[2] = lax.optimization_barrier((rest[3], far_rest[2]))
    far_rest.append(move(rest[3], swap_far))
    rest_core.append(move(far_rest[2], swap_c))

    def start(block):
        shape = jax.ShapeDtypeStruct((rows, cols), jnp.float32)
        return block, call(early_kernel, shape, name="early")(block, mine_all, other_all)

    def finish(block, early, i):
        chunks, places = PARTS[i]
        widths = [HD * sum(out == j for out, _ in places) for j in range(2)]
        shapes = [jax.ShapeDtypeStruct((rows, n), jnp.float32) for n in widths if n > 0]
        return call(lambda *refs: late_kernel(chunks, places, *refs), shapes, name="late")(
            block, early, *[far_rest[j] for j in chunks], *[rest_core[j] for j in chunks]
        )

    def send(part):
        return move(part.astype(jnp.float16), swap_near)

    far_part = start(far_block)
    part, kv_part = finish(*far_part, 0)
    kv_sum, sums = move(kv_part, swap_near), [send(part)]
    near_block = normed((here_near, *near_rows, stamped))
    near_block, far_rest, rest_core, kv_sum, sums = lax.optimization_barrier(
        (near_block, far_rest, rest_core, kv_sum, sums)
    )
    sums.append(send(finish(*far_part, 1)[0]))
    rest_core.append(move(far_rest[3], swap_c))
    part = finish(*far_part, 2)[0]
    sums.append(send(part))
    near_block, part = lax.optimization_barrier((near_block, part))

    def to_owner(z, x, y, c):
        return None if x == c else (z, c, y, x)

    widths = [[HD * sum(i == j for i, _ in places) for j in range(2)] for _, places in PARTS]
    part, kv_part, *parts = call(
        whole_kernel,
        [jax.ShapeDtypeStruct((rows, n), jnp.float32) for ns in widths for n in ns if n > 0],
        name="whole",
    )(near_block, mine_all, other_all, *far_rest, *rest_core)
    parts = [part, *parts]
    k_rot, v_val = call(
        keys_kernel, [jax.ShapeDtypeStruct((rows, HD), bf16)] * 2, name="keys"
    )(kv_part, kv_sum, cosine, sine)
    outs = [
        call(attend_kernel, jax.ShapeDtypeStruct(part.shape, bf16), name="attend")(
            part, got.astype(jnp.float32), cosine, sine, k_rot, v_val
        )
        for part, got in zip(parts, sums)
    ]
    came = [move(out, to_owner) for out in outs]
    return call(place_kernel, jax.ShapeDtypeStruct((rows, q_weight.shape[1] // 4), bf16), name="place")(
        *outs, *came
    )


def solution(mesh):
    placed = (
        P("batch", "tensor"),
        P("tensor"),
        P(("batch", "tensor"), None),
        P(("batch", "tensor"), None),
        P(("batch", "tensor"), None),
    )
    plan = split_plan if dict(mesh.shape) == {"batch": 8, "tensor": 4} else gathered_plan
    return jax.shard_map(
        plan, mesh=mesh, in_specs=placed, out_specs=P("batch", "tensor"), check_vma=False
    )
```

```python
import jax
import jax.numpy as jnp
from jax import lax
from jax.experimental import pallas as pl
from jax.experimental.pallas import tpu as pltpu
from jax.sharding import PartitionSpec as P

HD = 128
AXES = ("batch", "tensor")


def rotary_tables(seq_len, head_size):
    half = head_size // 2
    position = jnp.arange(seq_len, dtype=jnp.float32)
    freqs = 500000.0 ** (-(jnp.arange(half, dtype=jnp.float32) * 2.0) / head_size)
    angles = position[:, None] * freqs[None, :]
    return jnp.cos(angles), jnp.sin(angles)


def rotate_heads(field, tables):
    seq_len = field.shape[0]
    shaped = field.reshape(seq_len, -1, HD)
    half = HD // 2
    cosine = tables[0][:, None, :]
    sine = tables[1][:, None, :]
    first = shaped[..., :half]
    second = shaped[..., half:]
    turned = jnp.concatenate(
        [first * cosine - second * sine, second * cosine + first * sine], axis=-1
    )
    return turned.astype(jnp.bfloat16)


def attend(q_rot, k_rot, v_val):
    seq_len = q_rot.shape[0]
    scores = jnp.einsum("shd,td->hst", q_rot, k_rot, preferred_element_type=jnp.float32) / jnp.sqrt(
        jnp.float32(HD)
    )
    causal = jnp.tril(jnp.ones((seq_len, seq_len), dtype=bool))
    scores = jnp.where(causal[None], scores, jnp.float32(-1e30))
    top = jnp.max(scores, axis=-1, keepdims=True)
    expo = jnp.exp(scores - top)
    probs = (expo / jnp.sum(expo, axis=-1, keepdims=True)).astype(jnp.bfloat16)
    result = jnp.einsum("hst,td->shd", probs, v_val, preferred_element_type=jnp.float32)
    return result.astype(jnp.bfloat16).reshape(seq_len, -1)


def gathered_plan(hidden_in, norm_gain, q_weight, k_weight, v_weight):
    tensor_count = lax.axis_size("tensor")
    whole_rows, whole_gain = (
        lax.all_gather(hidden_in, "tensor", axis=1, tiled=True),
        lax.all_gather(norm_gain, "tensor", axis=0, tiled=True),
    )
    values = whole_rows.astype(jnp.float32)
    meansq = jnp.mean(values * values, axis=-1, keepdims=True)
    normed = (values * lax.rsqrt(meansq + 1e-05) * whole_gain.astype(jnp.float32)).astype(
        jnp.bfloat16
    )
    own_rows = q_weight.shape[0]
    kv_heads = k_weight.shape[1] // HD
    repeat_count = tensor_count // kv_heads
    q_send = q_weight.reshape(own_rows, tensor_count, -1)
    k_send = jnp.repeat(k_weight.reshape(own_rows, kv_heads, HD), repeat_count, axis=1)
    v_send = jnp.repeat(v_weight.reshape(own_rows, kv_heads, HD), repeat_count, axis=1)
    sends = jnp.concatenate([k_send, v_send, q_send], axis=2)
    recv = lax.all_to_all(sends, "tensor", split_axis=1, concat_axis=0, tiled=True)
    full = lax.all_gather(recv.reshape(-1, recv.shape[2]), "batch", axis=0, tiled=True)
    lin = jnp.dot(normed, full, preferred_element_type=jnp.float32)
    tables = rotary_tables(normed.shape[0], HD)
    k_rot = rotate_heads(lin[:, :HD], tables)[:, 0, :]
    v_val = lin[:, HD : 2 * HD].astype(jnp.bfloat16)
    return attend(rotate_heads(lin[:, 2 * HD :], tables), k_rot, v_val)


def move(value, route):
    pairs = []
    for flat in range(32):
        to = route(flat >> 3, flat >> 2 & 1, flat >> 1 & 1, flat & 1)
        if to is not None:
            pairs.append((flat, ((to[0] * 2 + to[1]) * 2 + to[2]) * 2 + to[3]))
    return lax.ppermute(value, AXES, pairs)


def swap_x(z, x, y, c):
    return z, 1 - x, y, c


def swap_y(z, x, y, c):
    return z, x, 1 - y, c


def swap_xy(z, x, y, c):
    return z, 1 - x, 1 - y, c


def swap_c(z, x, y, c):
    return z, x, y, 1 - c


def swap_near(z, x, y, c):
    return z ^ 1, x, y, c


def swap_far(z, x, y, c):
    return z ^ 2, x, y, c


CHUNKS = ((0, 3), (3, 5), (5, 8), (8, 10))
PARTS = (
    ((0, 1), ((1, 0), (1, 1), (0, 0), (0, 1), (0, 2))),
    ((2,), ((0, 0), (0, 1), (0, 2))),
    ((3,), ((0, 0), (0, 1))),
)
VMEM = {
    "pack": 8, "squares": 6, "stamp": 6, "rest": 10, "scale_rows": 16, "early": 15,
    "late": 14, "whole": 22, "attend": 10, "place": 5,
}


def place():
    batch, tensor = lax.axis_index("batch"), lax.axis_index("tensor")
    return batch >> 1, batch & 1, tensor >> 1, tensor & 1


def pick(pair, index):
    return lax.dynamic_index_in_dim(pair, index, 0, keepdims=False)


def call(kernel, out_shape, name=None, flops=0):
    shapes = out_shape if isinstance(out_shape, (list, tuple)) else (out_shape,)
    size = sum(2 * s.size * s.dtype.itemsize for s in shapes)
    return pl.pallas_call(
        kernel,
        out_shape=out_shape,
        compiler_params=pltpu.CompilerParams(vmem_limit_bytes=VMEM[name] * 2**20),
        cost_estimate=pl.CostEstimate(flops=flops, bytes_accessed=size, transcendentals=0),
        name=name,
    )


def pack_kernel(q_ref, k_ref, v_ref, *outs):
    _, x, y, _ = place()
    q_cols = outs[0].shape[1] - 2 * HD
    for out, px, py in zip(outs, (x, 1 - x, x, 1 - x), (y, y, 1 - y, 1 - y)):
        group = 2 * py + px
        out[:, :HD] = k_ref[:, pl.ds(pl.multiple_of(group * HD, HD), HD)]
        out[:, HD : 2 * HD] = v_ref[:, pl.ds(pl.multiple_of(group * HD, HD), HD)]
        out[:, 2 * HD :] = q_ref[:, pl.ds(pl.multiple_of(group * q_cols, HD), q_cols)]


def rest_kernel(own_ref, a_ref, b_ref, c_ref, far_ref, all_ref, *outs):
    own = a_ref.shape[0]
    for i, ref in enumerate((own_ref, a_ref, b_ref, c_ref, far_ref)):
        all_ref[i * own : (i + 1) * own, :] = ref[...]
        for out, (lo, hi) in zip(outs, CHUNKS):
            if 0 < i < 4:
                out[(i - 1) * own : i * own, :] = ref[:, lo * HD : hi * HD]


def squares_kernel(rows_ref, out):
    value = rows_ref[...].astype(jnp.float32)
    total = jnp.sum(value * value, axis=1, keepdims=True)
    out[...] = jnp.transpose(jnp.broadcast_to(total, (total.shape[0], HD)))[: out.shape[0], :]


def stamp_kernel(rows_ref, gain_ref, own_ref, got_ref, out):
    rows, feats = rows_ref.shape
    out[:rows, :] = rows_ref[...]
    left = own_ref[...] + got_ref[...]
    parts = []
    for _ in range(3):
        part = left.astype(jnp.bfloat16).astype(jnp.float32)
        parts.append(part)
        left = left - part
    parts.append(jnp.zeros((left.shape[0], feats - 3 * rows), jnp.float32))
    tile = jnp.concatenate(parts, axis=1)
    at = lax.broadcasted_iota(jnp.int32, tile.shape, 0)
    tile = jnp.where(at == 0, gain_ref[...].astype(jnp.float32), tile)
    out[rows:, :] = jnp.concatenate([tile, tile], axis=0).astype(jnp.bfloat16)


def scale_kernel(here, by_x, by_y, by_xy, *refs):
    z, x, y, c = place()
    out = refs[-1]
    rows, feats = out.shape[0], here.shape[1]
    own = feats // 8
    near = y == z >> 1
    home = jnp.logical_and(len(refs) > 1, c == z & 1)
    kept = refs[0] if len(refs) > 1 else here

    def fill(same, other):
        tiles = [ref[rows:, :].astype(jnp.float32) for ref in (same, other)]
        total = sum(tile[1:2, i * rows : (i + 1) * rows] for tile in tiles for i in range(3))
        scale = lax.rsqrt(total / (4 * feats) + 1e-05)
        scale = jnp.transpose(jnp.broadcast_to(scale, (HD, rows)))[:, :1]
        for ref, tile, is_near in (
            (same, tiles[0], near), (other, tiles[1], jnp.logical_not(near))
        ):
            for i in range(8):
                span = slice(i * own, (i + 1) * own)
                core = (i & 1) ^ c
                piece = (i >> 2 ^ x) + 2 * (i >> 1 & 1 ^ y)
                at_far = jnp.where(piece == 0, 5 * core + 4, 9 + 3 * core + piece)
                at = jnp.where(is_near, 5 * core + piece, at_far)
                to = pl.ds(pl.multiple_of(at * own, own), own)
                value = ref[:rows, span].astype(jnp.float32) * scale * tile[:1, span]
                out[:, to] = value.astype(jnp.bfloat16)

    @pl.when(jnp.logical_and(c == x, jnp.logical_not(home)))
    def _():
        fill(here, by_y)

    @pl.when(jnp.logical_and(c == x, home))
    def _():
        fill(kept, by_y)

    @pl.when(c != x)
    def _():
        fill(by_x, by_xy)


def dot(a, b):
    return jnp.dot(a, b, preferred_element_type=jnp.float32)


def early_kernel(lhs, *refs):
    total, at = 0.0, 0
    for ref in refs[:-1]:
        total = total + dot(lhs[:, at : at + ref.shape[0]], ref[...])
        at += ref.shape[0]
    refs[-1][...] = total


def late_kernel(chunks, places, lhs, early, *refs):
    count = len(chunks)
    outs = refs[2 * count :]
    places = iter(places)
    for j, rest, rest_core in zip(chunks, refs[:count], refs[count : 2 * count]):
        depth = rest.shape[0]
        start = lhs.shape[1] - 2 * depth
        lo, hi = CHUNKS[j]
        got = dot(lhs[:, start : start + depth], rest[...])
        got = got + dot(lhs[:, start + depth :], rest_core[...]) + early[:, lo * HD : hi * HD]
        for h in range(hi - lo):
            i, at = next(places)
            outs[i][:, at * HD : (at + 1) * HD] = got[:, h * HD : (h + 1) * HD]


def whole_kernel(lhs, kv_sum, cos_ref, sin_ref, mine, other, *refs):
    count = len(CHUNKS)
    rest, rest_core, outs = refs[:count], refs[count : 2 * count], list(refs[2 * count :])
    depth = mine.shape[0]
    near = dot(lhs[:, :depth], mine[...]) + dot(lhs[:, depth : 2 * depth], other[...])
    for chunks, places in PARTS:
        parts = [outs.pop(0) for _ in range(1 + 2 * max(i for i, _ in places))]
        places = iter(places)
        for j in chunks:
            lo, hi = CHUNKS[j]
            got, at = near[:, lo * HD : hi * HD], 2 * depth
            for ref in (rest[j], rest_core[j]):
                got = got + dot(lhs[:, at : at + ref.shape[0]], ref[...])
                at += ref.shape[0]
            for h in range(hi - lo):
                i, to = next(places)
                head, at = got[:, h * HD : (h + 1) * HD], slice(to * HD, (to + 1) * HD)
                if i == 0:
                    parts[0][:, at] = head
                elif to == 0:
                    parts[1][...] = turn(head + kv_sum[:, at], cos_ref[...], sin_ref[...])
                else:
                    parts[2][...] = (head + kv_sum[:, at]).astype(jnp.bfloat16)


def place_kernel(*refs):
    _, x, _, c = place()
    out = refs[-1]
    count = len(refs) // 2

    def fill(parts):
        at = 0
        for ref in parts:
            out[:, at : at + ref.shape[1]] = ref[...]
            at += ref.shape[1]

    @pl.when(c == x)
    def _():
        fill(refs[:count])

    @pl.when(c != x)
    def _():
        fill(refs[count:-1])


def turn(value, cosine, sine):
    return (value * cosine + pltpu.roll(value, HD // 2, 1) * sine).astype(jnp.bfloat16)


def attend_kernel(near_ref, got_ref, cos_ref, sin_ref, k_ref, v_ref, out_ref):
    rows, width = out_ref.shape
    half = rows // 2
    cosine, sine = cos_ref[...], sin_ref[...]
    spans = [slice(h, h + HD) for h in range(0, width, HD)]
    queries = [turn(near_ref[:, span] + got_ref[:, span], cosine, sine) for span in spans]
    scale = 1.4426950408889634 / HD**0.5
    for lo, hi in ((0, half), (half, rows)):
        mine = jnp.concatenate([q[lo:hi] for q in queries], axis=0)
        scores = lax.dot_general(
            mine, k_ref[:hi, :], (((1,), (1,)), ((), ())), preferred_element_type=jnp.float32
        )
        row = lax.broadcasted_iota(jnp.int32, (half, hi), 0) + lo
        later = lax.broadcasted_iota(jnp.int32, (half, hi), 1) > row
        probs = []
        for h in range(len(spans)):
            s = jnp.where(later, -1e30, scores[h * half : (h + 1) * half])
            expo = jnp.exp2((s - jnp.max(s, axis=1, keepdims=True)) * scale)
            inverse = 1.0 / jnp.sum(expo, axis=1, keepdims=True)
            probs.append((expo * inverse).astype(jnp.bfloat16))
        got = dot(jnp.concatenate(probs, axis=0), v_ref[:hi, :]).astype(jnp.bfloat16)
        for h, span in enumerate(spans):
            out_ref[lo:hi, span] = got[h * half : (h + 1) * half]


def split_plan(hidden_in, norm_gain, q_weight, k_weight, v_weight):
    z, x, y, c = place()
    home = c == z & 1
    direct = c == x
    rows, feats = hidden_in.shape
    own = q_weight.shape[0]
    cols = (q_weight.shape[1] + k_weight.shape[1] + v_weight.shape[1]) // 4
    bf16 = jnp.bfloat16

    mine, for_x, for_y, for_xy = call(
        pack_kernel, [jax.ShapeDtypeStruct((own, cols), bf16)] * 4, name="pack"
    )(q_weight, k_weight, v_weight)
    def to_other_plane(z, x, y, c):
        return None if c == z & 1 else (z ^ 1, x, y, x)

    def to_core(z, x, y, c):
        return (z, x, y, x) if c == z & 1 and c != x else None

    squares = call(squares_kernel, jax.ShapeDtypeStruct((8, rows), jnp.float32), name="squares")(
        hidden_in
    )
    stamped = call(stamp_kernel, jax.ShapeDtypeStruct((rows + 16, feats), bf16), name="stamp")(
        hidden_in, norm_gain[None, :], squares, move(squares, swap_c)
    )
    here_far = move(stamped, to_other_plane)
    far_mine = move(mine, swap_far)
    pieces = (move(for_x, swap_x), move(for_y, swap_y), move(for_xy, swap_xy))
    mine, far_mine, pieces = lax.optimization_barrier((mine, far_mine, pieces))
    mine_all, *rest = call(
        rest_kernel,
        [jax.ShapeDtypeStruct((5 * own, cols), bf16)]
        + [jax.ShapeDtypeStruct((3 * own, (hi - lo) * HD), bf16) for lo, hi in CHUNKS],
        name="rest",
    )(mine, *pieces, far_mine)

    def give_far(dx, dy):
        return lambda z, x, y, c: (z, x ^ dx, y ^ dy, c) if c == x else None

    def give_near(dx, dy):
        return lambda z, x, y, c: (z, x ^ dx, y ^ dy, x) if c == z & 1 else None

    def spread(block, give):
        return [move(block, give(1, 0)), move(block, give(0, 1)), move(block, give(1, 1))]

    def normed(blocks):
        shape = jax.ShapeDtypeStruct((rows, 2 * feats), bf16)
        return call(scale_kernel, shape, name="scale_rows", flops=2 * 10**10)(*blocks)

    here_far, rest, mine_all = lax.optimization_barrier((here_far, rest, mine_all))
    far_rows = [here_far, *spread(here_far, give_far)]
    far_rest = [move(rest[0], swap_far)]
    rest[1], far_rest[0] = lax.optimization_barrier((rest[1], far_rest[0]))
    far_rest.append(move(rest[1], swap_far))
    cosine, sine = rotary_tables(rows, HD)
    cosine = jnp.concatenate([cosine, cosine], axis=1)
    sine = jnp.concatenate([-sine, sine], axis=1)
    other_all, here_near = move(mine_all, swap_c), move(stamped, to_core)
    rest_core = [move(far_rest[0], swap_c)]
    far_block = normed(far_rows)
    far_block, far_rest, rest_core, stamped, here_near, other_all, rest[2], cosine, sine = (
        lax.optimization_barrier(
            (far_block, far_rest, rest_core, stamped, here_near, other_all, rest[2], cosine, sine)
        )
    )

    near_rows = spread(stamped, give_near)
    far_rest.append(move(rest[2], swap_far))
    rest_core.append(move(far_rest[1], swap_c))
    rest[3], far_rest[2] = lax.optimization_barrier((rest[3], far_rest[2]))
    far_rest.append(move(rest[3], swap_far))
    rest_core.append(move(far_rest[2], swap_c))

    def start(block):
        shape = jax.ShapeDtypeStruct((rows, cols), jnp.float32)
        return block, call(early_kernel, shape, name="early")(block, mine_all, other_all)

    def finish(block, early, i):
        chunks, places = PARTS[i]
        widths = [HD * sum(out == j for out, _ in places) for j in range(2)]
        shapes = [jax.ShapeDtypeStruct((rows, n), jnp.float32) for n in widths if n > 0]
        return call(lambda *refs: late_kernel(chunks, places, *refs), shapes, name="late")(
            block, early, *[far_rest[j] for j in chunks], *[rest_core[j] for j in chunks]
        )

    def send(part):
        return move(part.astype(jnp.float16), swap_near)

    far_part = start(far_block)
    part, kv_part = finish(*far_part, 0)
    kv_sum, sums = move(kv_part, swap_near), [send(part)]
    near_block = normed((here_near, *near_rows, stamped))
    near_block, far_rest, rest_core, kv_sum, sums = lax.optimization_barrier(
        (near_block, far_rest, rest_core, kv_sum, sums)
    )
    sums.append(send(finish(*far_part, 1)[0]))
    rest_core.append(move(far_rest[3], swap_c))
    part = finish(*far_part, 2)[0]
    sums.append(send(part))
    near_block, part = lax.optimization_barrier((near_block, part))

    def to_owner(z, x, y, c):
        return None if x == c else (z, c, y, x)

    widths = [[HD * sum(i == j for i, _ in places) for j in range(2)] for _, places in PARTS]
    shapes = [jax.ShapeDtypeStruct((rows, ns[0]), jnp.float32) for ns in widths]
    shapes[1:1] = [jax.ShapeDtypeStruct((rows, HD), bf16)] * 2
    part, k_rot, v_val, *parts = call(whole_kernel, shapes, name="whole")(
        near_block, kv_sum, cosine, sine, mine_all, other_all, *far_rest, *rest_core
    )
    parts = [part, *parts]
    outs = [
        call(attend_kernel, jax.ShapeDtypeStruct(part.shape, bf16), name="attend")(
            part, got.astype(jnp.float32), cosine, sine, k_rot, v_val
        )
        for part, got in zip(parts, sums)
    ]
    came = [move(out, to_owner) for out in outs]
    return call(place_kernel, jax.ShapeDtypeStruct((rows, q_weight.shape[1] // 4), bf16), name="place")(
        *outs, *came
    )


def solution(mesh):
    placed = (
        P("batch", "tensor"),
        P("tensor"),
        P(("batch", "tensor"), None),
        P(("batch", "tensor"), None),
        P(("batch", "tensor"), None),
    )
    plan = split_plan if dict(mesh.shape) == {"batch": 8, "tensor": 4} else gathered_plan
    return jax.shard_map(
        plan, mesh=mesh, in_specs=placed, out_specs=P("batch", "tensor"), check_vma=False
    )
```
